256 devices in a mesh: dp: 16 (over y, x_lo, core), ctx: 16 (over x_hi, z).
Axes of the slice: x: 4 (x_hi: 2, x_lo: 2; x = x_hi * 2 + x_lo), y: 4, z: 8, core: 2. Of those that a mesh axis runs over, the one named last changes fastest.
Arguments:
- q_long: bfloat16 [16, 4096, 768], P('dp', 'ctx'), may hold values from -8 to 8
- k_long: bfloat16 [16, 4096, 128], P('dp', 'ctx'), may hold values from -8 to 8
- v_long: bfloat16 [16, 4096, 128], P('dp', 'ctx'), may hold values from -6 to 6
- o_long: bfloat16 [16, 4096, 768], P('dp', 'ctx'), may hold values from -4 to 4
- dout_long: bfloat16 [16, 4096, 768], P('dp', 'ctx'), may hold values from -6 to 6
- doc_lengths: int32 [16, 4], P('dp'), may hold values from 1 to 2048, 4096 in all within a row
- q_short: bfloat16 [16, 64, 128, 768], P('dp', 'ctx'), may hold values from -8 to 8
- k_short: bfloat16 [16, 64, 128, 128], P('dp', 'ctx'), may hold values from -8 to 8
- v_short: bfloat16 [16, 64, 128, 128], P('dp', 'ctx'), may hold values from -6 to 6
- o_short: bfloat16 [16, 64, 128, 768], P('dp', 'ctx'), may hold values from -4 to 4
- dout_short: bfloat16 [16, 64, 128, 768], P('dp', 'ctx'), may hold values from -6 to 6
- short_len: int32 [16, 64], P('dp', 'ctx'), may hold values from 1 to 128, as said below
- short_count: int32 [16, 16], P('dp', 'ctx'), may hold values from 0 to 4, as said below
Outputs:
- dq_long: bfloat16 [16, 4096, 768], P('dp', 'ctx')
- dk_long: bfloat16 [16, 4096, 128], P('dp', 'ctx')
- dv_long: bfloat16 [16, 4096, 128], P('dp', 'ctx')
- dq_short: bfloat16 [16, 64, 128, 768], P('dp', 'ctx')
- dk_short: bfloat16 [16, 64, 128, 128], P('dp', 'ctx')
- dv_short: bfloat16 [16, 64, 128, 128], P('dp', 'ctx')
The draws below stay inside these ranges and needn't reach their ends.
Inputs may be any that keep to these rules, and one draw needn't show every extreme that they name: `doc_lengths`: each row sums to 4096; its longest document has exactly 2048 tokens. `short_count`: for each index of the second dimension the counts over the first dimension sum to exactly 32, and some device holds 4 live slots. `short_len`: some live slot holds a document of 128 rows; lengths of slots that are not live are ignored.
All inputs are finite; a program needn't handle non-finite values.
Results may differ from the reference program's by a relative error of at most 0.0085.
Values may be sent and summed in bfloat16 or wider, within the bound.
A program may use at most 128 MiB of HBM per device.

```python
import math
import jax
import jax.numpy as jnp
import numpy as np
from jax import lax

H = 6
DH = 128
TOK_DEV = 256
NDOC = 4
SL = 128
BAL = 2
SSLOT = 4
SEQS = 16
SEQ = 4096
SHORT = 64
N_CTX = 16


def drawn_rows(key, shape):
    return jnp.clip(jax.random.normal(key, shape, jnp.float32), -6.0, 6.0)


def draw_q_long(key, part):
    key = jax.random.fold_in(key, 11)
    shape = (SEQS, TOK_DEV * N_CTX, H * DH)
    return drawn_rows(key, shape).astype(jnp.bfloat16)


def draw_k_long(key, part):
    key = jax.random.fold_in(key, 13)
    shape = (SEQS, TOK_DEV * N_CTX, DH)
    return drawn_rows(key, shape).astype(jnp.bfloat16)


def draw_q_short(key, part):
    key = jax.random.fold_in(key, 17)
    shape = (SEQS, SSLOT * N_CTX, SL, H * DH)
    return drawn_rows(key, shape).astype(jnp.bfloat16)


def draw_k_short(key, part):
    key = jax.random.fold_in(key, 19)
    shape = (SEQS, SSLOT * N_CTX, SL, DH)
    return drawn_rows(key, shape).astype(jnp.bfloat16)


def draw_short_count(key, part):
    key = jax.random.fold_in(key, 23)
    half_count = SEQS // 2

    def column(column_key):
        order = jax.random.permutation(jax.random.fold_in(column_key, 1), SEQS)
        surplus = jax.random.randint(jax.random.fold_in(column_key, 2), (half_count,), 0, BAL + 1)
        surplus = surplus.at[0].set(BAL)
        counts = jnp.concatenate([BAL + surplus, BAL - surplus]).astype(jnp.int32)
        return jnp.zeros((SEQS,), jnp.int32).at[order].set(counts)
    column_keys = jax.random.split(key, N_CTX)
    return jnp.transpose(jax.vmap(column)(column_keys)).astype(jnp.int32)


def draw_short_len(key, part):
    key = jax.random.fold_in(key, 29)
    lengths = jax.random.randint(jax.random.fold_in(key, 1), (SEQS, SSLOT * N_CTX), 1, SL + 1)
    picked = jax.random.randint(jax.random.fold_in(key, 2), (SEQS, N_CTX), 0, 2)
    slot_index = jnp.arange(SSLOT * N_CTX)
    full_slot = slot_index[None, :] % SSLOT == picked[:, slot_index // SSLOT]
    return jnp.where(full_slot, SL, lengths).astype(jnp.int32)


def steps_of(rng, shape, cuts, low, high):
    gain = 1.0
    for dim, parts in cuts:
        steps = jax.random.uniform(jax.random.fold_in(jax.random.fold_in(rng, 6), dim), (parts,), jnp.float32, low / len(cuts), high / len(cuts))
        gain = gain * jnp.repeat(jnp.exp(steps), shape[dim] // parts).reshape((-1,) + (1,) * (len(shape) - 1 - dim))
    return gain


def split_up(number_of, total, limit, lean):
    loads = [(1 << 20) // math.isqrt(standing ** lean) + 1 for standing in range(2, number_of + 1)]
    spare, holding = total - limit - (number_of - 1), [1] * (number_of - 1)
    while spare > 0:
        candidates = [i for i in range(number_of - 1) if holding[i] < limit]
        mass, left = sum([loads[i] for i in candidates]), spare
        for i in candidates:
            extra = min(limit - holding[i], max(1, left * loads[i] // mass), spare)
            holding[i] = holding[i] + extra
            spare = spare - extra
    return np.array([limit] + holding)


def ragged_sizes(stream_key, number_of, total, limit, slope):
    if number_of == 2:
        one = jax.random.randint(stream_key, (), max(1, total - limit), min(limit, total - 1) + 1)
        return jnp.stack([one, total - one])
    tallies = jnp.asarray(split_up(number_of, total, limit, slope), jnp.int32)
    twos = (number_of - 1) // 2
    source_of, sink = tallies[1:1 + 2 * twos:2], tallies[2:2 + 2 * twos:2]
    slack = jnp.minimum(source_of - 1, limit - sink)
    passed = jax.random.randint(jax.random.fold_in(stream_key, 1), (twos,), 0, 1 << 20) % (slack + 1)
    tallies = tallies.at[1:1 + 2 * twos:2].set(source_of - passed).at[2:2 + 2 * twos:2].set(sink + passed)
    return tallies[jax.random.permutation(jax.random.fold_in(stream_key, 2), number_of)]


def gaussian(stream_key, shape, deviation, bound, shards=(), kind=jnp.bfloat16):
    level = steps_of(stream_key, shape, shards, -0.22, 0.18) if shards else 1.0
    entries = jax.random.normal(stream_key, shape, jnp.float32) * deviation * level
    return jnp.minimum(jnp.maximum(entries, -bound), bound).astype(kind)


def setup_inputs(seed: int = 0) -> dict:
    arg_keys = jax.random.split(jax.random.key(seed), 14)
    return {
        "q_long": draw_q_long(jax.random.fold_in(arg_keys[13], 71), 0),
        "k_long": draw_k_long(jax.random.fold_in(arg_keys[13], 71), 0),
        "v_long": gaussian(arg_keys[2], (SEQS, SEQ, DH), 1.0, 6.0, ((0, 16), (1, 16))),
        "o_long": gaussian(arg_keys[3], (SEQS, SEQ, H * DH), 0.5, 4.0, ((0, 16), (1, 16))),
        "dout_long": gaussian(arg_keys[4], (SEQS, SEQ, H * DH), 1.0, 6.0, ((0, 16), (1, 16))),
        "doc_lengths": jax.vmap(lambda own: ragged_sizes(own, NDOC, SEQ, SEQ // 2, 2))(jax.random.split(arg_keys[5], SEQS)).reshape((SEQS, NDOC)).astype(jnp.int32),
        "q_short": draw_q_short(jax.random.fold_in(arg_keys[13], 71), 0),
        "k_short": draw_k_short(jax.random.fold_in(arg_keys[13], 71), 0),
        "v_short": gaussian(arg_keys[8], (SEQS, SHORT, SL, DH), 1.0, 6.0, ((0, 16), (1, 16))),
        "o_short": gaussian(arg_keys[9], (SEQS, SHORT, SL, H * DH), 0.5, 4.0, ((0, 16), (1, 16))),
        "dout_short": gaussian(arg_keys[10], (SEQS, SHORT, SL, H * DH), 1.0, 6.0, ((0, 16), (1, 16))),
        "short_len": draw_short_len(jax.random.fold_in(arg_keys[13], 71), 0),
        "short_count": draw_short_count(jax.random.fold_in(arg_keys[13], 71), 0),
    }


big_negative = -1e+30

def stored_positions(row_index, shard_rows, shard_count):
    half_rows = shard_rows // 2
    owner_shard = row_index // shard_rows
    within = row_index % shard_rows
    early_pos = owner_shard * half_rows + within
    late_pos = (2 * shard_count - 1 - owner_shard) * half_rows + within - half_rows
    return jnp.where(within < half_rows, early_pos, late_pos).astype(jnp.int32)

def documents_of(positions, lengths):
    doc_ends = jnp.cumsum(lengths).astype(jnp.int32)
    return lax.optimization_barrier(jnp.sum((positions[:, None] >= doc_ends[None, :]).astype(jnp.int32), axis=1)).astype(jnp.int32)

def long_sequence(operands):
    queries, key_rows, value_rows, outputs, grad_out, lengths = operands
    seq_rows = queries.shape[0]
    score_scale = 1.0 / math.sqrt(DH)
    all_pos = stored_positions(jnp.arange(seq_rows, dtype=jnp.int32), TOK_DEV, N_CTX)
    all_docs = documents_of(all_pos, lengths)
    query_heads = queries.astype(jnp.float32).reshape(seq_rows, H, DH)
    grad_heads = grad_out.astype(jnp.float32).reshape(seq_rows, H, DH)
    out_heads = outputs.astype(jnp.float32).reshape(seq_rows, H, DH)
    key_float = key_rows.astype(jnp.float32)
    value_float = value_rows.astype(jnp.float32)
    query_block = min(seq_rows, 512)
    block_total = seq_rows // query_block

    def one_block(carried, block_number):
        key_grad, value_grad = carried
        first_row = block_number * query_block
        block_query = lax.dynamic_slice_in_dim(query_heads, first_row, query_block, 0)
        block_grad = lax.dynamic_slice_in_dim(grad_heads, first_row, query_block, 0)
        block_out = lax.dynamic_slice_in_dim(out_heads, first_row, query_block, 0)
        block_pos = lax.dynamic_slice_in_dim(all_pos, first_row, query_block, 0)
        block_docs = lax.dynamic_slice_in_dim(all_docs, first_row, query_block, 0)
        visible_mask = ((block_docs[:, None] == all_docs[None, :]) & (all_pos[None, :] <= block_pos[:, None]))[None]
        scores = jnp.einsum('ihd,jd->hij', block_query, key_float) * score_scale
        row_max = lax.optimization_barrier(jnp.max(jnp.where(visible_mask, scores, big_negative), axis=2, keepdims=True))
        weights = jnp.where(visible_mask, jnp.exp(scores - row_max), 0.0)
        probs = weights / lax.optimization_barrier(jnp.sum(weights, axis=2, keepdims=True))
        probs_round = lax.optimization_barrier(probs.astype(jnp.bfloat16)).astype(jnp.float32)
        delta = jnp.transpose(lax.optimization_barrier(jnp.sum(block_grad * block_out, axis=2)))[:, :, None]
        dprobs = jnp.einsum('ihd,jd->hij', block_grad, value_float)
        dscores = lax.optimization_barrier((probs * (dprobs - delta)).astype(jnp.bfloat16)).astype(jnp.float32)
        query_grad = jnp.einsum('hij,jd->ihd', dscores, key_float) * score_scale
        key_grad = key_grad + jnp.einsum('hij,ihd->jd', dscores, block_query) * score_scale
        value_grad = value_grad + jnp.einsum('hij,ihd->jd', probs_round, block_grad)
        return ((key_grad, value_grad), query_grad.reshape(query_block, H * DH).astype(jnp.bfloat16))
    zero_rows = jnp.zeros((seq_rows, DH), jnp.float32)
    (key_grad, value_grad), query_grads = lax.scan(one_block, (zero_rows, zero_rows), jnp.arange(block_total, dtype=jnp.int32))
    return (query_grads.reshape(seq_rows, H * DH), key_grad.astype(jnp.bfloat16), value_grad.astype(jnp.bfloat16))

def short_slots(queries, key_rows, value_rows, outputs, grad_out, lengths):
    slot_total = queries.shape[0]
    slot_rows = queries.shape[1]
    score_scale = 1.0 / math.sqrt(DH)
    query_heads = queries.astype(jnp.float32).reshape(slot_total, slot_rows, H, DH)
    grad_heads = grad_out.astype(jnp.float32).reshape(slot_total, slot_rows, H, DH)
    out_heads = outputs.astype(jnp.float32).reshape(slot_total, slot_rows, H, DH)
    key_float = key_rows.astype(jnp.float32)
    value_float = value_rows.astype(jnp.float32)
    row_index = jnp.arange(slot_rows, dtype=jnp.int32)
    live_rows = row_index[None, :] < lengths[:, None]
    causal = (row_index[None, :] <= row_index[:, None])[None]
    visible_mask = (causal & live_rows[:, None, :] & live_rows[:, :, None])[:, None]
    scores = jnp.einsum('bihd,bjd->bhij', query_heads, key_float) * score_scale
    row_max = lax.optimization_barrier(jnp.max(jnp.where(visible_mask, scores, big_negative), axis=3, keepdims=True))
    weights = jnp.where(visible_mask, jnp.exp(scores - row_max), 0.0)
    row_sum = lax.optimization_barrier(jnp.sum(weights, axis=3, keepdims=True))
    row_sum = jnp.where(live_rows[:, None, :, None], row_sum, 1.0)
    probs = weights / row_sum
    probs_round = lax.optimization_barrier(probs.astype(jnp.bfloat16)).astype(jnp.float32)
    delta = jnp.transpose(lax.optimization_barrier(jnp.sum(grad_heads * out_heads, axis=3)), (0, 2, 1))[:, :, :, None]
    dprobs = jnp.einsum('bihd,bjd->bhij', grad_heads, value_float)
    dscores = lax.optimization_barrier((probs * (dprobs - delta)).astype(jnp.bfloat16)).astype(jnp.float32)
    query_grad = jnp.einsum('bhij,bjd->bihd', dscores, key_float) * score_scale
    key_grad = jnp.einsum('bhij,bihd->bjd', dscores, query_heads) * score_scale
    value_grad = jnp.einsum('bhij,bihd->bjd', probs_round, grad_heads)
    return (query_grad.reshape(slot_total, slot_rows, H * DH).astype(jnp.bfloat16), key_grad.astype(jnp.bfloat16), value_grad.astype(jnp.bfloat16))

def short_sequence(operands):
    queries, key_rows, value_rows, outputs, grad_out, lengths, counts = operands
    grads = short_slots(queries, key_rows, value_rows, outputs, grad_out, lengths)
    slot_index = jnp.arange(SSLOT * N_CTX, dtype=jnp.int32)
    live_slots = slot_index % SSLOT < counts[slot_index // SSLOT]
    return tuple((jnp.where(live_slots[:, None, None], grad_part, jnp.zeros_like(grad_part)) for grad_part in grads))

def reference(q_long, k_long, v_long, o_long, dout_long, doc_lengths, q_short, k_short, v_short, o_short, dout_short, short_len, short_count):
    dq_long, dk_long, dv_long = lax.map(long_sequence, (q_long, k_long, v_long, o_long, dout_long, doc_lengths))
    dq_short, dk_short, dv_short = lax.map(short_sequence, (q_short, k_short, v_short, o_short, dout_short, short_len, short_count))
    return (dq_long, dk_long, dv_long, dq_short, dk_short, dv_short)
```

```python
import math

import jax
import jax.numpy as jnp
from jax import lax
from jax.experimental import pallas as pl
from jax.experimental.pallas import tpu as pltpu
from jax.sharding import PartitionSpec as P

H = 6
DH = 128
CH = 128
NZ = 8
NCTX = 16
NCHUNK = 32
NDOC = 4
SLOTS = 4
HC = H * DH
PAIRS = tuple(range(0, HC, 2 * DH))
SCALE = 1.0 / math.sqrt(DH)
SCALE2 = SCALE * math.log2(math.e)
NEG = -1e30
ROOT_STEP = 0
LAST_STEP = 4

HOPS_UP = {
    (0, 0, 0): (3, 3, 3, 4, 3, 2, 1, 0),
    (0, 0, 1): (0, 0, 0, 0, 0, 4, 4, 4),
    (0, 1, 0): (0, 0, 3, 4, 3, 2, 4, 4),
    (0, 1, 1): (4, 3, 4, 3, 4, 3, 4, 3),
    (1, 0, 0): (4, 4, 4, 4, 4, 4, 4, 4),
    (1, 0, 1): (0, 0, 0, 0, 0, 4, 4, 4),
    (1, 1, 0): (4, 3, 4, 3, 4, 3, 4, 3),
    (1, 1, 1): (0, 0, 0, 0, 0, 0, 0, 0),
}
HOPS_DOWN = {
    (0, 0, 0): (4, 4, 4, 0, 0, 0, 0, 0),
    (0, 0, 1): (0, 1, 2, 3, 4, 3, 3, 3),
    (0, 1, 0): (1, 3, 4, 0, 1, 3, 3, 3),
    (0, 1, 1): (3, 4, 3, 4, 3, 4, 3, 4),
    (1, 0, 0): (3, 3, 3, 3, 3, 3, 3, 3),
    (1, 0, 1): (0, 1, 2, 3, 4, 3, 3, 3),
    (1, 1, 0): (3, 4, 3, 4, 3, 4, 3, 4),
    (1, 1, 1): (0, 0, 0, 0, 0, 0, 0, 0),
}


def packed(hops):
    return sum(h << (3 * z) for z, h in enumerate(hops))


def nt(a, b):
    return lax.dot_general(a, b, (((1,), (1,)), ((), ())), preferred_element_type=jnp.float32)


def nn(a, b):
    return lax.dot_general(a, b, (((1,), (0,)), ((), ())), preferred_element_type=jnp.float32)


def heads(ref, col):
    return jnp.concatenate([ref[:, col : col + DH], ref[:, col + DH : col + 2 * DH]], axis=0)


def row_delta(grads, outs):
    prod = grads.astype(jnp.float32) * outs.astype(jnp.float32)
    high = prod.astype(jnp.bfloat16)
    low = (prod - high.astype(jnp.float32)).astype(jnp.bfloat16)
    ones = jnp.ones((16, DH), jnp.bfloat16)
    return (nt(ones, high) + nt(ones, low))[0:1]


def kernel(
    q_hbm, k_hbm, v_hbm, o_hbm, do_hbm, doc_ref,
    qs_hbm, ks_hbm, vs_hbm, os_hbm, dos_hbm, slen_ref, scount_ref,
    dq_hbm, dk_hbm, dv_hbm, dqs_hbm, dks_hbm, dvs_hbm,
    kv, q_v, o_v, do_v, scores, m_v, l_v, delta_v, lo_v, dqt, acc, own,
    snd, rcv, rcvx, qs_v, ks_v, vs_v, os_v, dos_v, dq_v, dkv_v, dqs_v, dks_v, dvs_v,
    in_sem, out_sem, ag_send, ag_recv, rs_send, rs_recv, rsx_recv,
):
    f32, bf16 = jnp.float32, jnp.bfloat16
    c = lax.axis_index("ctx")
    x = c // NZ
    z = c - x * NZ
    late_own = 2 * NCTX - 1 - c
    z_up = lax.rem(z + 1, NZ)
    z_down = lax.rem(z + NZ - 1, NZ)
    across = (1 - x) * NZ + z
    beside = (x * NZ + z_up, x * NZ + z_down)

    def hops(direction, foreign, late, z_root):
        table = (HOPS_UP, HOPS_DOWN)[direction]
        code = jnp.where(x == 1, packed(table[1, foreign, late]), packed(table[0, foreign, late]))
        return (code >> (3 * z_root)) & 7

    def hops_dynamic(direction, foreign, late, z_root):
        up = [[hops(0, f, l, z_root) for l in (0, 1)] for f in (0, 1)]
        down = [[hops(1, f, l, z_root) for l in (0, 1)] for f in (0, 1)]
        pick = lambda t: jnp.where(
            foreign == 1, jnp.where(late == 1, t[1][1], t[1][0]), jnp.where(late == 1, t[0][1], t[0][0])
        )
        return jnp.where(direction == 1, pick(down), pick(up))

    def chunk_of(foreign, late, z_root):
        owner = jnp.where(foreign == 1, 1 - x, x) * NZ + z_root
        return jnp.where(late == 1, 2 * NCTX - 1 - owner, owner)

    def early_needs(j):
        return j <= c

    def late_needs(j):
        return (j >= 15 - c) & (j <= late_own)

    def ag_copy(j, way, target):
        return pltpu.make_async_remote_copy(
            src_ref=kv.at[j], dst_ref=kv.at[j], send_sem=ag_send.at[j, way], recv_sem=ag_recv.at[j],
            device_id={"ctx": target}, device_id_type=pl.DeviceIdType.MESH,
        )

    def rs_copy(j, way, target):
        return pltpu.make_async_remote_copy(
            src_ref=snd.at[j], dst_ref=rcv.at[way, j], send_sem=rs_send.at[j], recv_sem=rs_recv.at[way, j],
            device_id={"ctx": target}, device_id_type=pl.DeviceIdType.MESH,
        )

    def rsx_copy(j, late):
        return pltpu.make_async_remote_copy(
            src_ref=snd.at[j], dst_ref=rcvx.at[late], send_sem=rs_send.at[j], recv_sem=rsx_recv.at[late],
            device_id={"ctx": across}, device_id_type=pl.DeviceIdType.MESH,
        )

    kv_loads = [
        pltpu.make_async_copy(src.at[0, pl.ds(half * CH, CH)], kv.at[j, which], in_sem.at[2 * which + half])
        for which, src in ((0, k_hbm), (1, v_hbm))
        for half, j in ((0, c), (1, late_own))
    ]
    long_loads = [
        pltpu.make_async_copy(src.at[0], dst, in_sem.at[4 + n])
        for n, (src, dst) in enumerate(((q_hbm, q_v), (do_hbm, do_v), (o_hbm, o_v)))
    ]
    short_loads = [
        pltpu.make_async_copy(src.at[0], dst, in_sem.at[7 + n])
        for n, (src, dst) in enumerate(
            ((qs_hbm, qs_v), (ks_hbm, ks_v), (vs_hbm, vs_v), (os_hbm, os_v), (dos_hbm, dos_v))
        )
    ]
    for copy in kv_loads + long_loads + short_loads:
        copy.start()

    barrier = pltpu.get_barrier_semaphore()
    for target in beside + (across,):
        pl.semaphore_signal(
            barrier, inc=1, device_id={"ctx": target}, device_id_type=pl.DeviceIdType.MESH
        )
    pl.semaphore_wait(barrier, 3)

    def crosses(late):
        return (x == 1) | (late == 0)

    def arrives(late):
        return (x == 0) | (late == 0)

    for copy in kv_loads:
        copy.wait()
    for late in (0, 1):
        j = chunk_of(0, late, z)

        @pl.when(crosses(late))
        def _():
            ag_copy(j, 2, across).start()

    for late in (0, 1):
        j = chunk_of(0, late, z)
        for way in (0, 1):

            @pl.when(hops(way, 0, late, z) >= 1)
            def _():
                ag_copy(j, way, beside[way]).start()

    for copy in long_loads:
        copy.wait()
    halves = [(pl.ds(half * CH, CH), own_chunk) for half, own_chunk in ((0, c), (1, late_own))]
    ends = []
    total = doc_ref[0, 0]
    for d in range(NDOC):
        ends.append(total)
        if d + 1 < NDOC:
            total = total + doc_ref[0, d + 1]
    lane = lax.rem(lax.broadcasted_iota(jnp.int32, (1, 2 * DH), 1), CH)
    sub = lax.broadcasted_iota(jnp.int32, (CH, 1), 0)
    for half, (rows, own_chunk) in enumerate(halves):
        pos = own_chunk * CH + lane
        first = jnp.zeros((1, 2 * DH), jnp.int32)
        for end in ends:
            first = jnp.maximum(first, jnp.where(pos >= end, end, 0))
        lo_v[half] = first
        for col in PAIRS:
            delta_v[half, :, col : col + 2 * DH] = row_delta(heads(do_v.at[rows], col), heads(o_v.at[rows], col))
        m_v[half] = jnp.full((1, HC), NEG, f32)
        l_v[half] = jnp.zeros((1, HC), f32)
        dqt[half] = jnp.zeros((DH, HC), f32)

    def slot_of(half, j):
        return j if half == 0 else NCTX + j - (15 - c)

    def score_tile(half, j):
        rows, own_chunk = halves[half]
        keys = kv[j, 0]
        key_pos = j * CH + sub
        visible = (key_pos >= lo_v[half]) & (key_pos <= own_chunk * CH + lane)
        slot = slot_of(half, j)
        for col in PAIRS:
            cols = slice(col, col + 2 * DH)
            s = nt(keys, heads(q_v.at[rows], col)) * SCALE2
            s = jnp.where(visible, s, NEG)
            scores[slot, :, cols] = s
            m_old = m_v[half, :, cols]
            m_new = jnp.maximum(m_old, jnp.max(s, axis=0, keepdims=True))
            l_v[half, :, cols] = l_v[half, :, cols] * jnp.exp2(m_old - m_new) + jnp.sum(
                jnp.exp2(s - m_new), axis=0, keepdims=True
            )
            m_v[half, :, cols] = m_new

    def score_item(j, has):
        @pl.when(has & early_needs(j))
        def _():
            score_tile(0, j)

        @pl.when(has & late_needs(j))
        def _():
            score_tile(1, j)

    def short_slot(slot):
        length = jnp.where(slot < scount_ref[0, 0], slen_ref[0, slot], 0)
        keys = ks_v[slot]
        values = vs_v[slot]
        visible = (sub <= lane) & (lane < length)
        dk = jnp.zeros((CH, DH), f32)
        dv = jnp.zeros((CH, DH), f32)
        for col in PAIRS:
            queries = heads(qs_v.at[slot], col)
            grads = heads(dos_v.at[slot], col)
            delta = row_delta(grads, heads(os_v.at[slot], col))
            s = jnp.where(visible, nt(keys, queries) * SCALE2, NEG)
            e = jnp.exp2(s - jnp.max(s, axis=0, keepdims=True))
            inverse = jnp.where(lane < length, 1.0 / jnp.sum(e, axis=0, keepdims=True), 0.0)
            p = e * inverse
            ds = (p * (nt(values, grads) - delta)).astype(bf16)
            dv = dv + nn(p.astype(bf16), grads)
            dk = dk + nn(ds, queries)
            dq = lax.dot_general(keys, ds, (((0,), (0,)), ((), ())), preferred_element_type=f32)
            for n in (0, 1):
                dqs_v[slot, :, col + n * DH : col + (n + 1) * DH] = (
                    dq[:, n * DH : (n + 1) * DH].T * SCALE
                ).astype(bf16)
        dks_v[slot] = (dk * SCALE).astype(bf16)
        dvs_v[slot] = dv.astype(bf16)

    score_item(c, c >= 0)
    score_item(late_own, c >= 0)

    for late in (0, 1):
        j = chunk_of(1, late, z)

        @pl.when(arrives(late))
        def _():
            ag_copy(j, 2, across).wait_recv()
            for way in (0, 1):

                @pl.when(hops(way, 1, late, z) >= 1)
                def _():
                    ag_copy(j, way, beside[way]).start()

    def foreign_score(late, carry):
        score_item(chunk_of(1, late, z), arrives(late))
        return carry

    lax.fori_loop(0, 2, foreign_score, 0)

    for copy in short_loads:
        copy.wait()

    def gather_step(step, carry):
        for foreign in (0, 1):
            for late in (0, 1):
                for way in (0, 1):
                    z_root = lax.rem(z + NZ + (step if way == 1 else -step), NZ)
                    j = chunk_of(foreign, late, z_root)
                    reach = hops(way, foreign, late, z_root)

                    @pl.when(reach >= step)
                    def _():
                        ag_copy(j, way, beside[way]).wait_recv()

                    @pl.when(reach >= step + 1)
                    def _():
                        ag_copy(j, way, beside[way]).start()

        short_slot(step - 1)

        def item(n, carry):
            foreign, late, way = n // 4, lax.rem(n // 2, 2), lax.rem(n, 2)
            z_root = lax.rem(z + NZ + jnp.where(way == 1, step, -step), NZ)
            score_item(chunk_of(foreign, late, z_root), hops_dynamic(way, foreign, late, z_root) >= step)
            return carry

        return lax.fori_loop(0, 8, item, carry)

    lax.fori_loop(1, LAST_STEP + 1, gather_step, 0)

    short_stores = [
        pltpu.make_async_copy(src, dst.at[0], out_sem.at[n])
        for n, (src, dst) in enumerate(((dqs_v, dqs_hbm), (dks_v, dks_hbm), (dvs_v, dvs_hbm)))
    ]
    for copy in short_stores:
        copy.start()

    for half in (0, 1):
        m_v[half] = m_v[half] + jnp.log2(l_v[half])

    def grad_tile(half, j):
        rows, own_chunk = halves[half]
        keys = kv[j, 0]
        values = kv[j, 1]
        slot = slot_of(half, j)
        dk = acc[0]
        dv = acc[1]
        for col in PAIRS:
            cols = slice(col, col + 2 * DH)
            queries = heads(q_v.at[rows], col)
            grads = heads(do_v.at[rows], col)
            p = jnp.exp2(scores[slot, :, cols] - m_v[half, :, cols])
            ds = (p * (nt(values, grads) - delta_v[half, :, cols])).astype(bf16)
            dv = dv + nn(p.astype(bf16), grads)
            dk = dk + nn(ds, queries)
            dqt[half, :, cols] += lax.dot_general(
                keys, ds, (((0,), (0,)), ((), ())), preferred_element_type=f32
            )
        acc[0] = dk
        acc[1] = dv

    def grad_item(j):
        acc[...] = jnp.zeros((2, CH, DH), f32)

        @pl.when(early_needs(j))
        def _():
            grad_tile(0, j)

        @pl.when(late_needs(j))
        def _():
            grad_tile(1, j)

    def scatter_step(back, carry):
        step = LAST_STEP - back

        def item(n, carry):
            foreign, late, way = n // 4, lax.rem(n // 2, 2), lax.rem(n, 2)
            z_root = lax.rem(z + NZ + jnp.where(way == 1, step, -step), NZ)
            j = chunk_of(foreign, late, z_root)
            reach = hops_dynamic(way, foreign, late, z_root)

            @pl.when(reach >= step)
            def _():
                grad_item(j)
                home = jnp.where(way == 1, beside[0], beside[1])
                copy = rs_copy(j, way, home)

                @pl.when(reach >= step + 1)
                def _():
                    copy.wait_recv()
                    acc[...] += rcv[way, j].astype(f32)

                snd[j] = acc[...].astype(bf16)
                copy.start()

            return carry

        return lax.fori_loop(0, 8, item, carry)

    lax.fori_loop(0, LAST_STEP, scatter_step, 0)

    def collect(foreign, late, j):
        for way in (0, 1):

            @pl.when(hops_dynamic(way, foreign, late, z) >= 1)
            def _():
                rs_copy(j, way, beside[way]).wait_recv()
                acc[...] += rcv[way, j].astype(f32)

    def foreign_root(late, carry):
        j = chunk_of(1, late, z)

        @pl.when(arrives(late))
        def _():
            grad_item(j)
            collect(1, late, j)
            snd[j] = acc[...].astype(bf16)
            rsx_copy(j, late).start()

        return carry

    lax.fori_loop(0, 2, foreign_root, 0)

    def own_root(late, carry):
        grad_item(chunk_of(0, late, z))
        own[late] = acc[...]
        return carry

    lax.fori_loop(0, 2, own_root, 0)

    for half, (rows, own_chunk) in enumerate(halves):
        for col in range(0, HC, DH):
            dq_v[rows, col : col + DH] = (dqt[half, :, col : col + DH].T * SCALE).astype(bf16)
    dq_store = pltpu.make_async_copy(dq_v, dq_hbm.at[0], out_sem.at[3])
    dq_store.start()

    def own_total(late, carry):
        acc[...] = own[late]
        j = chunk_of(0, late, z)
        collect(0, late, j)

        @pl.when(crosses(late))
        def _():
            rsx_copy(j, late).wait_recv()
            acc[...] += rcvx[late].astype(f32)

        rows = pl.ds(pl.multiple_of(late * CH, CH), CH)
        dkv_v[0, rows] = (acc[0] * SCALE).astype(bf16)
        dkv_v[1, rows] = acc[1].astype(bf16)
        return carry

    lax.fori_loop(0, 2, own_total, 0)
    kv_stores = [
        pltpu.make_async_copy(dkv_v.at[n], dst.at[0], out_sem.at[4 + n]) for n, dst in enumerate((dk_hbm, dv_hbm))
    ]
    for copy in kv_stores:
        copy.start()

    for late in (0, 1):
        j = chunk_of(0, late, z)

        @pl.when(crosses(late))
        def _():
            ag_copy(j, 2, across).wait_send()

        for foreign in (0, 1):
            j = chunk_of(foreign, late, z)
            for way in (0, 1):

                @pl.when(hops(way, foreign, late, z) >= 1)
                def _():
                    ag_copy(j, way, beside[way]).wait_send()

        @pl.when(arrives(late))
        def _():
            rsx_copy(chunk_of(1, late, z), late).wait_send()

    def sent_step(step, carry):
        def item(n, carry):
            foreign, late, way = n // 4, lax.rem(n // 2, 2), lax.rem(n, 2)
            z_root = lax.rem(z + NZ + jnp.where(way == 1, step, -step), NZ)
            j = chunk_of(foreign, late, z_root)
            reach = hops_dynamic(way, foreign, late, z_root)

            @pl.when(reach >= step)
            def _():
                rs_copy(j, way, beside[0]).wait_send()

            @pl.when(reach >= step + 1)
            def _():
                ag_copy(j, way, beside[0]).wait_send()

            return carry

        return lax.fori_loop(0, 8, item, carry)

    lax.fori_loop(1, LAST_STEP + 1, sent_step, 0)

    for copy in short_stores + [dq_store] + kv_stores:
        copy.wait()


def body(*args):
    bf16, f32 = jnp.bfloat16, jnp.float32
    tok = args[0].shape[1]
    any_spec = pl.BlockSpec(memory_space=pl.ANY)
    smem_spec = pl.BlockSpec(memory_space=pltpu.SMEM)
    in_specs = [any_spec] * 5 + [smem_spec] + [any_spec] * 5 + [smem_spec] * 2
    out_shape = [jax.ShapeDtypeStruct(args[n].shape, bf16) for n in (0, 1, 2, 6, 7, 8)]
    dma = pltpu.SemaphoreType.DMA
    scratch = [
        pltpu.VMEM((NCHUNK, 2, CH, DH), bf16),
        pltpu.VMEM((tok, HC), bf16),
        pltpu.VMEM((tok, HC), bf16),
        pltpu.VMEM((tok, HC), bf16),
        pltpu.VMEM((33, CH, HC), f32),
        pltpu.VMEM((2, 1, HC), f32),
        pltpu.VMEM((2, 1, HC), f32),
        pltpu.VMEM((2, 1, HC), f32),
        pltpu.VMEM((2, 1, 2 * DH), jnp.int32),
        pltpu.VMEM((2, DH, HC), f32),
        pltpu.VMEM((2, CH, DH), f32),
        pltpu.VMEM((2, 2, CH, DH), f32),
        pltpu.VMEM((NCHUNK, 2, CH, DH), bf16),
        pltpu.VMEM((2, NCHUNK, 2, CH, DH), bf16),
        pltpu.VMEM((2, 2, CH, DH), bf16),
        pltpu.VMEM((SLOTS, CH, HC), bf16),
        pltpu.VMEM((SLOTS, CH, DH), bf16),
        pltpu.VMEM((SLOTS, CH, DH), bf16),
        pltpu.VMEM((SLOTS, CH, HC), bf16),
        pltpu.VMEM((SLOTS, CH, HC), bf16),
        pltpu.VMEM((tok, HC), bf16),
        pltpu.VMEM((2, tok, DH), bf16),
        pltpu.VMEM((SLOTS, CH, HC), bf16),
        pltpu.VMEM((SLOTS, CH, DH), bf16),
        pltpu.VMEM((SLOTS, CH, DH), bf16),
        dma((12,)),
        dma((6,)),
        dma((NCHUNK, 3)),
        dma((NCHUNK,)),
        dma((NCHUNK,)),
        dma((2, NCHUNK)),
        dma((2,)),
    ]
    return tuple(
        pl.pallas_call(
            kernel,
            out_shape=out_shape,
            in_specs=in_specs,
            out_specs=[any_spec] * 6,
            scratch_shapes=scratch,
            compiler_params=pltpu.CompilerParams(
                collective_id=0, has_side_effects=True, vmem_limit_bytes=48 * 1024 * 1024
            ),
            name="attention_backward",
        )(*args)
    )


def solution(mesh):
    seq = P("dp", "ctx", None)
    slot = P("dp", "ctx", None, None)
    return jax.shard_map(
        body,
        mesh=mesh,
        in_specs=(seq,) * 5 + (P("dp", None),) + (slot,) * 5 + (P("dp", "ctx"),) * 2,
        out_specs=(seq, seq, seq, slot, slot, slot),
        check_vma=False,
    )
```

```python
import math

import jax
import jax.numpy as jnp
from jax import lax
from jax.experimental import pallas as pl
from jax.experimental.pallas import tpu as pltpu
from jax.sharding import PartitionSpec as P

H = 6
DH = 128
CH = 128
NZ = 8
NCTX = 16
NCHUNK = 32
NDOC = 4
SLOTS = 4
HC = H * DH
PAIRS = tuple(range(0, HC, 2 * DH))
SCALE = 1.0 / math.sqrt(DH)
SCALE2 = SCALE * math.log2(math.e)
NEG = -1e30
ROOT_STEP = 0
LAST_STEP = 4

HOPS_UP = {
    (0, 0, 0): (3, 3, 3, 4, 3, 2, 1, 0),
    (0, 0, 1): (0, 0, 0, 0, 0, 4, 4, 4),
    (0, 1, 0): (0, 0, 3, 4, 3, 2, 4, 4),
    (0, 1, 1): (4, 3, 4, 3, 4, 3, 4, 3),
    (1, 0, 0): (4, 4, 4, 4, 4, 4, 4, 4),
    (1, 0, 1): (0, 0, 0, 0, 0, 4, 4, 4),
    (1, 1, 0): (4, 3, 4, 3, 4, 3, 4, 3),
    (1, 1, 1): (0, 0, 0, 0, 0, 0, 0, 0),
}
HOPS_DOWN = {
    (0, 0, 0): (4, 4, 4, 0, 0, 0, 0, 0),
    (0, 0, 1): (0, 1, 2, 3, 4, 3, 3, 3),
    (0, 1, 0): (1, 3, 4, 0, 1, 3, 3, 3),
    (0, 1, 1): (3, 4, 3, 4, 3, 4, 3, 4),
    (1, 0, 0): (3, 3, 3, 3, 3, 3, 3, 3),
    (1, 0, 1): (0, 1, 2, 3, 4, 3, 3, 3),
    (1, 1, 0): (3, 4, 3, 4, 3, 4, 3, 4),
    (1, 1, 1): (0, 0, 0, 0, 0, 0, 0, 0),
}


def packed(hops):
    return sum(h << (3 * z) for z, h in enumerate(hops))


def nt(a, b):
    return lax.dot_general(a, b, (((1,), (1,)), ((), ())), preferred_element_type=jnp.float32)


def nn(a, b):
    return lax.dot_general(a, b, (((1,), (0,)), ((), ())), preferred_element_type=jnp.float32)


def heads(ref, col):
    return jnp.concatenate([ref[:, col : col + DH], ref[:, col + DH : col + 2 * DH]], axis=0)


def row_delta(grads, outs):
    prod = grads.astype(jnp.float32) * outs.astype(jnp.float32)
    high = prod.astype(jnp.bfloat16)
    low = (prod - high.astype(jnp.float32)).astype(jnp.bfloat16)
    ones = jnp.ones((16, DH), jnp.bfloat16)
    return (nt(ones, high) + nt(ones, low))[0:1]


def kernel(
    q_hbm, k_hbm, v_hbm, o_hbm, do_hbm, doc_ref,
    qs_hbm, ks_hbm, vs_hbm, os_hbm, dos_hbm, slen_ref, scount_ref,
    dq_hbm, dk_hbm, dv_hbm, dqs_hbm, dks_hbm, dvs_hbm,
    kv, q_v, o_v, do_v, scores, ds_v, m_v, l_v, lse_v, delta_v, lo_v, dqt, acc, own,
    snd, rcv, rcvx, qs_v, ks_v, vs_v, os_v, dos_v, dq_v, dkv_v, dqs_v, dks_v, dvs_v,
    in_sem, out_sem, ag_send, ag_recv, rs_send, rs_recv, rsx_recv,
):
    f32, bf16 = jnp.float32, jnp.bfloat16
    c = lax.axis_index("ctx")
    x = c // NZ
    z = c - x * NZ
    late_own = 2 * NCTX - 1 - c
    z_up = lax.rem(z + 1, NZ)
    z_down = lax.rem(z + NZ - 1, NZ)
    across = (1 - x) * NZ + z
    beside = (x * NZ + z_up, x * NZ + z_down)

    codes = [
        [
            [jnp.where(x == 1, packed(table[1, foreign, late]), packed(table[0, foreign, late])) for late in (0, 1)]
            for foreign in (0, 1)
        ]
        for table in (HOPS_UP, HOPS_DOWN)
    ]

    def hops(direction, foreign, late, z_root):
        code = codes[direction][foreign][late]
        return (code >> (3 * z_root)) & 7

    def hops_dynamic(direction, foreign, late, z_root):
        by_way = [[jnp.where(direction == 1, codes[1][f][l], codes[0][f][l]) for l in (0, 1)] for f in (0, 1)]
        by_late = [jnp.where(late == 1, both[1], both[0]) for both in by_way]
        return (jnp.where(foreign == 1, by_late[1], by_late[0]) >> (3 * z_root)) & 7

    def chunk_of(foreign, late, z_root):
        owner = jnp.where(foreign == 1, 1 - x, x) * NZ + z_root
        return jnp.where(late == 1, 2 * NCTX - 1 - owner, owner)

    def early_needs(j):
        return j <= c

    def late_needs(j):
        return (j >= 15 - c) & (j <= late_own)

    def ag_copy(j, way, target):
        return pltpu.make_async_remote_copy(
            src_ref=kv.at[j], dst_ref=kv.at[j], send_sem=ag_send.at[j, way], recv_sem=ag_recv.at[j],
            device_id={"ctx": target}, device_id_type=pl.DeviceIdType.MESH,
        )

    def rs_copy(j, way, target):
        return pltpu.make_async_remote_copy(
            src_ref=snd.at[j], dst_ref=rcv.at[way, j], send_sem=rs_send.at[j], recv_sem=rs_recv.at[way, j],
            device_id={"ctx": target}, device_id_type=pl.DeviceIdType.MESH,
        )

    def rsx_copy(j, late):
        return pltpu.make_async_remote_copy(
            src_ref=snd.at[j], dst_ref=rcvx.at[late], send_sem=rs_send.at[j], recv_sem=rsx_recv.at[late],
            device_id={"ctx": across}, device_id_type=pl.DeviceIdType.MESH,
        )

    kv_loads = [
        pltpu.make_async_copy(src.at[0, pl.ds(half * CH, CH)], kv.at[j, which], in_sem.at[2 * which + half])
        for which, src in ((0, k_hbm), (1, v_hbm))
        for half, j in ((0, c), (1, late_own))
    ]
    long_loads = [
        pltpu.make_async_copy(src.at[0], dst, in_sem.at[4 + n])
        for n, (src, dst) in enumerate(((q_hbm, q_v), (do_hbm, do_v), (o_hbm, o_v)))
    ]
    short_loads = [
        pltpu.make_async_copy(src.at[0], dst, in_sem.at[7 + n])
        for n, (src, dst) in enumerate(
            ((qs_hbm, qs_v), (ks_hbm, ks_v), (vs_hbm, vs_v), (os_hbm, os_v), (dos_hbm, dos_v))
        )
    ]
    for copy in kv_loads + long_loads + short_loads:
        copy.start()

    barrier = pltpu.get_barrier_semaphore()
    for target in beside + (across,):
        pl.semaphore_signal(
            barrier, inc=1, device_id={"ctx": target}, device_id_type=pl.DeviceIdType.MESH
        )
    pl.semaphore_wait(barrier, 3)

    def crosses(late):
        return (x == 1) | (late == 0)

    def arrives(late):
        return (x == 0) | (late == 0)

    for copy in kv_loads:
        copy.wait()
    for late in (0, 1):
        j = chunk_of(0, late, z)

        @pl.when(crosses(late))
        def _():
            ag_copy(j, 2, across).start()

    for late in (0, 1):
        j = chunk_of(0, late, z)
        for way in (0, 1):

            @pl.when(hops(way, 0, late, z) >= 1)
            def _():
                ag_copy(j, way, beside[way]).start()

    for copy in long_loads:
        copy.wait()
    halves = [(pl.ds(half * CH, CH), own_chunk) for half, own_chunk in ((0, c), (1, late_own))]
    ends = []
    total = doc_ref[0, 0]
    for d in range(NDOC):
        ends.append(total)
        if d + 1 < NDOC:
            total = total + doc_ref[0, d + 1]
    lane = lax.rem(lax.broadcasted_iota(jnp.int32, (1, 2 * DH), 1), CH)
    sub = lax.broadcasted_iota(jnp.int32, (CH, 1), 0)
    for half, (rows, own_chunk) in enumerate(halves):
        pos = own_chunk * CH + lane
        first = jnp.zeros((1, 2 * DH), jnp.int32)
        for end in ends:
            first = jnp.maximum(first, jnp.where(pos >= end, end, 0))
        lo_v[half] = first
        for col in PAIRS:
            delta_v[half, :, col : col + 2 * DH] = row_delta(heads(do_v.at[rows], col), heads(o_v.at[rows], col))
        m_v[half] = jnp.full((8, HC), NEG, f32)
        l_v[half] = jnp.zeros((8, HC), f32)
    dqt[0] = jnp.zeros((DH, HC), f32)

    def slot_of(half, j):
        return j if half == 0 else NCTX + j - (15 - c)

    def score_tiles(which, j):
        keys = kv[j, 0]
        key_pos = j * CH + sub
        for half in which:
            rows, own_chunk = halves[half]
            visible = (key_pos >= lo_v[half]) & (key_pos <= own_chunk * CH + lane)
            bias = jnp.where(visible, 0.0, NEG)
            slot = slot_of(half, j)
            for col in PAIRS:
                cols = slice(col, col + 2 * DH)
                s = nt(keys, heads(q_v.at[rows], col)) * SCALE2 + bias
                scores[slot, :, cols] = s
                s = s.reshape(CH // 8, 8, 2 * DH)
                m_old = m_v[half, :, cols]
                m_new = jnp.maximum(m_old, jnp.max(s, axis=0))
                m_v[half, :, cols] = m_new
                l_v[half, :, cols] = l_v[half, :, cols] * jnp.exp2(m_old - m_new) + jnp.sum(
                    jnp.exp2(s - m_new[None]), axis=0
                )

    def for_needed(j, has, tiles):
        early, late = early_needs(j), late_needs(j)
        for which, wanted in (((0, 1), early & late), ((0,), early & ~late), ((1,), late & ~early)):

            @pl.when(has & wanted)
            def _():
                tiles(which, j)

    def score_item(j, has):
        for_needed(j, has, score_tiles)

    def short_slot(slot):
        length = jnp.where(slot < scount_ref[0, 0], slen_ref[0, slot], 0)
        keys = ks_v[slot]
        values = vs_v[slot]
        visible = (sub <= lane) & (lane < length)
        dk = jnp.zeros((CH, DH), f32)
        dv = jnp.zeros((CH, DH), f32)
        for col in PAIRS:
            queries = heads(qs_v.at[slot], col)
            grads = heads(dos_v.at[slot], col)
            delta = row_delta(grads, heads(os_v.at[slot], col))
            s = jnp.where(visible, nt(keys, queries) * SCALE2, NEG)
            e = jnp.exp2(s - jnp.max(s, axis=0, keepdims=True))
            inverse = jnp.where(lane < length, 1.0 / jnp.sum(e, axis=0, keepdims=True), 0.0)
            p = e * inverse
            ds = (p * (nt(values, grads) - delta)).astype(bf16)
            dv = dv + nn(p.astype(bf16), grads)
            dk = dk + nn(ds, queries)
            dq = lax.dot_general(keys, ds, (((0,), (0,)), ((), ())), preferred_element_type=f32)
            for n in (0, 1):
                dqs_v[slot, :, col + n * DH : col + (n + 1) * DH] = (
                    dq[:, n * DH : (n + 1) * DH].T * SCALE
                ).astype(bf16)
        dks_v[slot] = (dk * SCALE).astype(bf16)
        dvs_v[slot] = dv.astype(bf16)

    score_item(c, c >= 0)
    score_item(late_own, c >= 0)

    for late in (0, 1):
        j = chunk_of(1, late, z)

        @pl.when(arrives(late))
        def _():
            ag_copy(j, 2, across).wait_recv()
            for way in (0, 1):

                @pl.when(hops(way, 1, late, z) >= 1)
                def _():
                    ag_copy(j, way, beside[way]).start()

    def foreign_score(late, carry):
        score_item(chunk_of(1, late, z), arrives(late))
        return carry

    lax.fori_loop(0, 2, foreign_score, 0)

    for copy in short_loads:
        copy.wait()

    def gather_step(step, carry):
        for foreign in (0, 1):
            for late in (0, 1):
                for way in (0, 1):
                    z_root = lax.rem(z + NZ + (step if way == 1 else -step), NZ)
                    j = chunk_of(foreign, late, z_root)
                    reach = hops(way, foreign, late, z_root)

                    @pl.when(reach >= step)
                    def _():
                        ag_copy(j, way, beside[way]).wait_recv()

                    @pl.when(reach >= step + 1)
                    def _():
                        ag_copy(j, way, beside[way]).start()

        short_slot(step - 1)

        def item(n, carry):
            foreign, late, way = n // 4, lax.rem(n // 2, 2), lax.rem(n, 2)
            z_root = lax.rem(z + NZ + jnp.where(way == 1, step, -step), NZ)
            score_item(chunk_of(foreign, late, z_root), hops_dynamic(way, foreign, late, z_root) >= step)
            return carry

        return lax.fori_loop(0, 8, item, carry)

    lax.fori_loop(1, LAST_STEP + 1, gather_step, 0)

    short_stores = [
        pltpu.make_async_copy(src, dst.at[0], out_sem.at[n])
        for n, (src, dst) in enumerate(((dqs_v, dqs_hbm), (dks_v, dks_hbm), (dvs_v, dvs_hbm)))
    ]
    for copy in short_stores:
        copy.start()

    for half in (0, 1):
        m = jnp.max(m_v[half], axis=0, keepdims=True)
        lse_v[half] = m + jnp.log2(jnp.sum(l_v[half] * jnp.exp2(m_v[half] - m), axis=0, keepdims=True))

    def grad_tiles(which, j):
        values = kv[j, 1]
        p_parts, ds_parts, q_parts, do_parts = [], [], [], []
        for half in which:
            rows, own_chunk = halves[half]
            slot = slot_of(half, j)
            for col in PAIRS:
                cols = slice(col, col + 2 * DH)
                grads = heads(do_v.at[rows], col)
                p = jnp.exp2(scores[slot, :, cols] - lse_v[half, :, cols])
                ds = (p * (nt(values, grads) - delta_v[half, :, cols])).astype(bf16)
                ds_v[slot, :, cols] = ds
                p_parts.append(p.astype(bf16))
                ds_parts.append(ds)
                q_parts.append(heads(q_v.at[rows], col))
                do_parts.append(grads)
        acc[0] = nn(jnp.concatenate(ds_parts, axis=1), jnp.concatenate(q_parts, axis=0))
        acc[1] = nn(jnp.concatenate(p_parts, axis=1), jnp.concatenate(do_parts, axis=0))

    def grad_item(j):
        @pl.when(~(early_needs(j) | late_needs(j)))
        def _():
            acc[...] = jnp.zeros((2, CH, DH), f32)

        for_needed(j, c >= 0, grad_tiles)

    def scatter_step(back, carry):
        step = LAST_STEP - back

        def item(n, carry):
            foreign, late, way = n // 4, lax.rem(n // 2, 2), lax.rem(n, 2)
            z_root = lax.rem(z + NZ + jnp.where(way == 1, step, -step), NZ)
            j = chunk_of(foreign, late, z_root)
            reach = hops_dynamic(way, foreign, late, z_root)

            @pl.when(reach >= step)
            def _():
                grad_item(j)
                home = jnp.where(way == 1, beside[0], beside[1])
                copy = rs_copy(j, way, home)

                @pl.when(reach >= step + 1)
                def _():
                    copy.wait_recv()
                    acc[...] += rcv[way, j].astype(f32)

                snd[j] = acc[...].astype(bf16)
                copy.start()

            return carry

        return lax.fori_loop(0, 8, item, carry)

    lax.fori_loop(0, LAST_STEP, scatter_step, 0)

    def collect(foreign, late, j):
        for way in (0, 1):

            @pl.when(hops_dynamic(way, foreign, late, z) >= 1)
            def _():
                rs_copy(j, way, beside[way]).wait_recv()
                acc[...] += rcv[way, j].astype(f32)

    def foreign_root(late, carry):
        j = chunk_of(1, late, z)

        @pl.when(arrives(late))
        def _():
            grad_item(j)
            collect(1, late, j)
            snd[j] = acc[...].astype(bf16)
            rsx_copy(j, late).start()

        return carry

    lax.fori_loop(0, 2, foreign_root, 0)

    def own_root(late, carry):
        grad_item(chunk_of(0, late, z))
        own[late] = acc[...]
        return carry

    lax.fori_loop(0, 2, own_root, 0)

    def tn(a, b):
        return lax.dot_general(a, b, (((0,), (0,)), ((), ())), preferred_element_type=f32)

    def dq_early(first, count):
        keys = kv[pl.ds(first, count), 0].reshape(count * CH, DH)
        for col in PAIRS:
            cols = slice(col, col + 2 * DH)
            dqt[0, :, cols] += tn(keys, ds_v[pl.ds(first, count), :, cols].reshape(count * CH, 2 * DH))

    def dq_early_two(n, carry):
        dq_early(2 * n, 2)
        return carry

    lax.fori_loop(0, (c + 1) // 2, dq_early_two, 0)

    @pl.when(lax.rem(c, 2) == 0)
    def _():
        dq_early(c, 1)

    keys = kv[pl.ds(15 - c, 17), 0].reshape(17 * CH, DH)
    for col in PAIRS:
        cols = slice(col, col + 2 * DH)
        dqt[1, :, cols] = tn(keys, ds_v[NCTX : NCTX + 17, :, cols].reshape(17 * CH, 2 * DH))
    for half, (rows, own_chunk) in enumerate(halves):
        for col in range(0, HC, DH):
            dq_v[rows, col : col + DH] = (dqt[half, :, col : col + DH].T * SCALE).astype(bf16)
    dq_store = pltpu.make_async_copy(dq_v, dq_hbm.at[0], out_sem.at[3])
    dq_store.start()

    def own_total(late, carry):
        acc[...] = own[late]
        j = chunk_of(0, late, z)
        collect(0, late, j)

        @pl.when(crosses(late))
        def _():
            rsx_copy(j, late).wait_recv()
            acc[...] += rcvx[late].astype(f32)

        rows = pl.ds(pl.multiple_of(late * CH, CH), CH)
        dkv_v[0, rows] = (acc[0] * SCALE).astype(bf16)
        dkv_v[1, rows] = acc[1].astype(bf16)
        return carry

    lax.fori_loop(0, 2, own_total, 0)
    kv_stores = [
        pltpu.make_async_copy(dkv_v.at[n], dst.at[0], out_sem.at[4 + n]) for n, dst in enumerate((dk_hbm, dv_hbm))
    ]
    for copy in kv_stores:
        copy.start()

    for late in (0, 1):
        j = chunk_of(0, late, z)

        @pl.when(crosses(late))
        def _():
            ag_copy(j, 2, across).wait_send()

        for foreign in (0, 1):
            j = chunk_of(foreign, late, z)
            for way in (0, 1):

                @pl.when(hops(way, foreign, late, z) >= 1)
                def _():
                    ag_copy(j, way, beside[way]).wait_send()

        @pl.when(arrives(late))
        def _():
            rsx_copy(chunk_of(1, late, z), late).wait_send()

    def sent_step(step, carry):
        def item(n, carry):
            foreign, late, way = n // 4, lax.rem(n // 2, 2), lax.rem(n, 2)
            z_root = lax.rem(z + NZ + jnp.where(way == 1, step, -step), NZ)
            j = chunk_of(foreign, late, z_root)
            reach = hops_dynamic(way, foreign, late, z_root)

            @pl.when(reach >= step)
            def _():
                rs_copy(j, way, beside[0]).wait_send()

            @pl.when(reach >= step + 1)
            def _():
                ag_copy(j, way, beside[0]).wait_send()

            return carry

        return lax.fori_loop(0, 8, item, carry)

    lax.fori_loop(1, LAST_STEP + 1, sent_step, 0)

    for copy in short_stores + [dq_store] + kv_stores:
        copy.wait()


def emit(*refs):
    sem = refs[12]
    copies = [pltpu.make_async_copy(refs[n], refs[6 + n], sem.at[n]) for n in range(6)]
    for copy in copies:
        copy.start()
    for copy in copies:
        copy.wait()


def body(*args):
    bf16, f32 = jnp.bfloat16, jnp.float32
    tok = args[0].shape[1]
    any_spec = pl.BlockSpec(memory_space=pltpu.HBM)
    smem_spec = pl.BlockSpec(memory_space=pltpu.SMEM)
    in_specs = [any_spec] * 5 + [smem_spec] + [any_spec] * 5 + [smem_spec] * 2
    out_shape = [jax.ShapeDtypeStruct(args[n].shape, bf16) for n in (0, 1, 2, 6, 7, 8)]
    dma = pltpu.SemaphoreType.DMA
    scratch = [
        pltpu.VMEM((NCHUNK, 2, CH, DH), bf16),
        pltpu.VMEM((tok, HC), bf16),
        pltpu.VMEM((tok, HC), bf16),
        pltpu.VMEM((tok, HC), bf16),
        pltpu.VMEM((33, CH, HC), f32),
        pltpu.VMEM((33, CH, HC), bf16),
        pltpu.VMEM((2, 8, HC), f32),
        pltpu.VMEM((2, 8, HC), f32),
        pltpu.VMEM((2, 1, HC), f32),
        pltpu.VMEM((2, 1, HC), f32),
        pltpu.VMEM((2, 1, 2 * DH), jnp.int32),
        pltpu.VMEM((2, DH, HC), f32),
        pltpu.VMEM((2, CH, DH), f32),
        pltpu.VMEM((2, 2, CH, DH), f32),
        pltpu.VMEM((NCHUNK, 2, CH, DH), bf16),
        pltpu.VMEM((2, NCHUNK, 2, CH, DH), bf16),
        pltpu.VMEM((2, 2, CH, DH), bf16),
        pltpu.VMEM((SLOTS, CH, HC), bf16),
        pltpu.VMEM((SLOTS, CH, DH), bf16),
        pltpu.VMEM((SLOTS, CH, DH), bf16),
        pltpu.VMEM((SLOTS, CH, HC), bf16),
        pltpu.VMEM((SLOTS, CH, HC), bf16),
        pltpu.VMEM((tok, HC), bf16),
        pltpu.VMEM((2, tok, DH), bf16),
        pltpu.VMEM((SLOTS, CH, HC), bf16),
        pltpu.VMEM((SLOTS, CH, DH), bf16),
        pltpu.VMEM((SLOTS, CH, DH), bf16),
        dma((12,)),
        dma((6,)),
        dma((NCHUNK, 3)),
        dma((NCHUNK,)),
        dma((NCHUNK,)),
        dma((2, NCHUNK)),
        dma((2,)),
    ]
    grads = pl.pallas_call(
        kernel,
        out_shape=out_shape,
        in_specs=in_specs,
        out_specs=[any_spec] * 6,
        scratch_shapes=scratch,
        compiler_params=pltpu.CompilerParams(
            collective_id=0, has_side_effects=True, vmem_limit_bytes=60 * 1024 * 1024
        ),
        name="attention_backward",
    )(*args)
    return tuple(
        pl.pallas_call(
            emit,
            out_shape=out_shape,
            in_specs=[any_spec] * 6,
            out_specs=[any_spec] * 6,
            scratch_shapes=[dma((6,))],
            compiler_params=pltpu.CompilerParams(vmem_limit_bytes=60 * 1024 * 1024),
            name="emit",
        )(*grads)
    )


def solution(mesh):
    seq = P("dp", "ctx", None)
    slot = P("dp", "ctx", None, None)
    return jax.shard_map(
        body,
        mesh=mesh,
        in_specs=(seq,) * 5 + (P("dp", None),) + (slot,) * 5 + (P("dp", "ctx"),) * 2,
        out_specs=(seq, seq, seq, slot, slot, slot),
        check_vma=False,
    )
```

```python
import math

import jax
import jax.numpy as jnp
from jax import lax
from jax.experimental import pallas as pl
from jax.experimental.pallas import tpu as pltpu
from jax.sharding import PartitionSpec as P

H = 6
DH = 128
CH = 128
NZ = 8
NCTX = 16
NCHUNK = 32
NDOC = 4
SLOTS = 4
HC = H * DH
PAIRS = tuple(range(0, HC, 2 * DH))
SCALE = 1.0 / math.sqrt(DH)
SCALE2 = SCALE * math.log2(math.e)
NEG = -1e30
LAST_STEP = 4

HOPS_UP = {
    (0, 0, 0): (4, 4, 4, 4, 4, 3, 1, 0),
    (0, 0, 1): (0, 0, 0, 0, 0, 4, 4, 4),
    (0, 1, 0): (0, 0, 0, 0, 0, 1, 1, 3),
    (0, 1, 1): (3, 3, 3, 3, 3, 0, 1, 2),
    (1, 0, 0): (4, 4, 3, 3, 4, 4, 4, 4),
    (1, 0, 1): (0, 0, 0, 0, 0, 3, 3, 4),
    (1, 1, 0): (0, 3, 4, 3, 3, 2, 4, 4),
    (1, 1, 1): (0, 0, 0, 0, 0, 0, 0, 0),
}
HOPS_DOWN = {
    (0, 0, 0): (3, 3, 3, 0, 3, 0, 0, 0),
    (0, 0, 1): (0, 1, 2, 3, 4, 3, 3, 3),
    (0, 1, 0): (1, 0, 0, 0, 0, 3, 0, 2),
    (0, 1, 1): (4, 4, 4, 4, 0, 3, 3, 0),
    (1, 0, 0): (3, 3, 4, 4, 3, 3, 3, 3),
    (1, 0, 1): (0, 1, 2, 3, 4, 4, 4, 3),
    (1, 1, 0): (3, 3, 0, 4, 0, 4, 3, 3),
    (1, 1, 1): (0, 0, 0, 0, 0, 0, 0, 0),
}


def packed(hops):
    return sum(h << (3 * z) for z, h in enumerate(hops))


def nt(a, b):
    return lax.dot_general(a, b, (((1,), (1,)), ((), ())), preferred_element_type=jnp.float32)


def nn(a, b):
    return lax.dot_general(a, b, (((1,), (0,)), ((), ())), preferred_element_type=jnp.float32)


def heads(ref, col):
    return jnp.concatenate([ref[:, col : col + DH], ref[:, col + DH : col + 2 * DH]], axis=0)


def row_delta(grads, outs):
    prod = grads.astype(jnp.float32) * outs.astype(jnp.float32)
    high = prod.astype(jnp.bfloat16)
    low = (prod - high.astype(jnp.float32)).astype(jnp.bfloat16)
    ones = jnp.ones((16, DH), jnp.bfloat16)
    return (nt(ones, high) + nt(ones, low))[0:1]


def kernel(
    q_hbm, k_hbm, v_hbm, o_hbm, do_hbm, doc_ref,
    qs_hbm, ks_hbm, vs_hbm, os_hbm, dos_hbm, slen_ref, scount_ref,
    dq_hbm, dk_hbm, dv_hbm, dqs_hbm, dks_hbm, dvs_hbm,
    kv, q_v, o_v, do_v, scores, ds_v, m_v, l_v, lse_v, delta_v, lo_v, dqt, acc, own,
    snd, rcv, qs_v, ks_v, vs_v, os_v, dos_v, dq_v, dkv_v, dqs_v, dks_v, dvs_v,
    in_sem, out_sem, ag_send, ag_recv, rs_send, rs_recv,
):
    f32, bf16 = jnp.float32, jnp.bfloat16
    c = lax.axis_index("ctx")
    x = c // NZ
    z = c - x * NZ
    late_own = 2 * NCTX - 1 - c
    z_up = lax.rem(z + 1, NZ)
    z_down = lax.rem(z + NZ - 1, NZ)
    across = (1 - x) * NZ + z
    beside = (x * NZ + z_up, x * NZ + z_down)

    def code(side, direction, foreign, late):
        table = (HOPS_UP, HOPS_DOWN)[direction]
        here, there = packed(table[0, foreign, late]), packed(table[1, foreign, late])
        return jnp.where(x == side, here, there)

    codes = [
        [[[code(side, direction, f, l) for l in (0, 1)] for f in (0, 1)] for direction in (0, 1)]
        for side in (0, 1)
    ]

    def choose(flag, one, zero):
        if isinstance(flag, int):
            return one if flag else zero
        return jnp.where(flag == 1, one, zero)

    def hops(direction, foreign, late, z_root, side=0):
        by_late = [
            [choose(late, codes[side][d][f][1], codes[side][d][f][0]) for f in (0, 1)] for d in (0, 1)
        ]
        by_foreign = [choose(foreign, both[1], both[0]) for both in by_late]
        return (choose(direction, by_foreign[1], by_foreign[0]) >> (3 * z_root)) & 7

    def chunk_of(foreign, late, z_root):
        owner = jnp.where(foreign == 1, 1 - x, x) * NZ + z_root
        return jnp.where(late == 1, 2 * NCTX - 1 - owner, owner)

    def early_needs(j, who=c):
        return j <= who

    def late_needs(j, who=c):
        return (j >= 15 - who) & (j <= 2 * NCTX - 1 - who)

    def needs(j, who):
        return early_needs(j, who) | late_needs(j, who)

    def root_of(way, step):
        return lax.rem(z + NZ + choose(way, step, -step), NZ)

    def comes_across(late, way, step):
        z_root = root_of(way, step)
        j = chunk_of(1, late, z_root)
        near, far = hops(way, 1, late, z_root), hops(1 - way, 1, late, z_root)
        there = hops(way, 0, late, z_root, side=1)
        return (there >= step) & (near < step) & (far < NZ - step) & needs(j, c)

    def goes_across(late, way, step):
        z_root = root_of(way, step)
        j = chunk_of(0, late, z_root)
        near, far = hops(way, 1, late, z_root, side=1), hops(1 - way, 1, late, z_root, side=1)
        here = hops(way, 0, late, z_root)
        return (here >= step) & (near < step) & (far < NZ - step) & needs(j, across)

    def ag_copy(j, way, target):
        return pltpu.make_async_remote_copy(
            src_ref=kv.at[j], dst_ref=kv.at[j], send_sem=ag_send.at[j, way], recv_sem=ag_recv.at[j],
            device_id={"ctx": target}, device_id_type=pl.DeviceIdType.MESH,
        )

    def rs_copy(j, way, target):
        return pltpu.make_async_remote_copy(
            src_ref=snd.at[j], dst_ref=rcv.at[way, j], send_sem=rs_send.at[j], recv_sem=rs_recv.at[way, j],
            device_id={"ctx": target}, device_id_type=pl.DeviceIdType.MESH,
        )

    kv_loads = [
        pltpu.make_async_copy(src.at[0, pl.ds(half * CH, CH)], kv.at[j, which], in_sem.at[2 * which + half])
        for which, src in ((0, k_hbm), (1, v_hbm))
        for half, j in ((0, c), (1, late_own))
    ]
    long_loads = [
        pltpu.make_async_copy(src.at[0], dst, in_sem.at[4 + n])
        for n, (src, dst) in enumerate(((q_hbm, q_v), (do_hbm, do_v), (o_hbm, o_v)))
    ]
    short_loads = [
        pltpu.make_async_copy(src.at[0], dst, in_sem.at[7 + n])
        for n, (src, dst) in enumerate(
            ((qs_hbm, qs_v), (ks_hbm, ks_v), (vs_hbm, vs_v), (os_hbm, os_v), (dos_hbm, dos_v))
        )
    ]
    for copy in kv_loads + long_loads + short_loads:
        copy.start()

    barrier = pltpu.get_barrier_semaphore()
    for target in beside + (across,):
        pl.semaphore_signal(
            barrier, inc=1, device_id={"ctx": target}, device_id_type=pl.DeviceIdType.MESH
        )
    pl.semaphore_wait(barrier, 3)

    def crosses(late):
        on = hops(0, 1, late, z, side=1) + hops(1, 1, late, z, side=1)
        return (on >= 1) | needs(chunk_of(0, late, z), across)

    def arrives(late):
        on = hops(0, 1, late, z) + hops(1, 1, late, z)
        return (on >= 1) | needs(chunk_of(1, late, z), c)

    for copy in kv_loads:
        copy.wait()
    for late in (0, 1):
        j = chunk_of(0, late, z)

        @pl.when(crosses(late))
        def _():
            ag_copy(j, 2, across).start()

    for late in (0, 1):
        j = chunk_of(0, late, z)
        for way in (0, 1):

            @pl.when(hops(way, 0, late, z) >= 1)
            def _():
                ag_copy(j, way, beside[way]).start()

    for copy in long_loads:
        copy.wait()
    halves = [(pl.ds(half * CH, CH), own_chunk) for half, own_chunk in ((0, c), (1, late_own))]
    ends = []
    total = doc_ref[0, 0]
    for d in range(NDOC):
        ends.append(total)
        if d + 1 < NDOC:
            total = total + doc_ref[0, d + 1]
    lane = lax.rem(lax.broadcasted_iota(jnp.int32, (1, 2 * DH), 1), CH)
    sub = lax.broadcasted_iota(jnp.int32, (CH, 1), 0)
    for half, (rows, own_chunk) in enumerate(halves):
        pos = own_chunk * CH + lane
        first = jnp.zeros((1, 2 * DH), jnp.int32)
        for end in ends:
            first = jnp.maximum(first, jnp.where(pos >= end, end, 0))
        lo_v[half] = first
        for col in PAIRS:
            delta_v[half, :, col : col + 2 * DH] = row_delta(heads(do_v.at[rows], col), heads(o_v.at[rows], col))
        m_v[half] = jnp.full((8, HC), NEG, f32)
        l_v[half] = jnp.zeros((8, HC), f32)
    dqt[0] = jnp.zeros((DH, HC), f32)

    def slot_of(half, j):
        return j if half == 0 else NCTX + j - (15 - c)

    def score_tiles(which, j):
        keys = kv[j, 0]
        key_pos = j * CH + sub
        for half in which:
            rows, own_chunk = halves[half]
            visible = (key_pos >= lo_v[half]) & (key_pos <= own_chunk * CH + lane)
            bias = jnp.where(visible, 0.0, NEG)
            slot = slot_of(half, j)
            for col in PAIRS:
                cols = slice(col, col + 2 * DH)
                s = nt(keys, heads(q_v.at[rows], col)) * SCALE2 + bias
                scores[slot, :, cols] = s
                s = s.reshape(CH // 8, 8, 2 * DH)
                m_old = m_v[half, :, cols]
                m_new = jnp.maximum(m_old, jnp.max(s, axis=0))
                m_v[half, :, cols] = m_new
                l_v[half, :, cols] = l_v[half, :, cols] * jnp.exp2(m_old - m_new) + jnp.sum(
                    jnp.exp2(s - m_new[None]), axis=0
                )

    def for_needed(j, has, tiles):
        early, late = early_needs(j), late_needs(j)
        for which, wanted in (((0, 1), early & late), ((0,), early & ~late), ((1,), late & ~early)):

            @pl.when(has & wanted)
            def _():
                tiles(which, j)

    def score_item(j, has):
        for_needed(j, has, score_tiles)

    def short_slot(slot):
        length = jnp.where(slot < scount_ref[0, 0], slen_ref[0, slot], 0)
        keys = ks_v[slot]
        values = vs_v[slot]
        visible = (sub <= lane) & (lane < length)
        dk = jnp.zeros((CH, DH), f32)
        dv = jnp.zeros((CH, DH), f32)
        for col in PAIRS:
            queries = heads(qs_v.at[slot], col)
            grads = heads(dos_v.at[slot], col)
            delta = row_delta(grads, heads(os_v.at[slot], col))
            s = jnp.where(visible, nt(keys, queries) * SCALE2, NEG)
            e = jnp.exp2(s - jnp.max(s, axis=0, keepdims=True))
            inverse = jnp.where(lane < length, 1.0 / jnp.sum(e, axis=0, keepdims=True), 0.0)
            p = e * inverse
            ds = (p * (nt(values, grads) - delta)).astype(bf16)
            dv = dv + nn(p.astype(bf16), grads)
            dk = dk + nn(ds, queries)
            dq = lax.dot_general(keys, ds, (((0,), (0,)), ((), ())), preferred_element_type=f32)
            for n in (0, 1):
                dqs_v[slot, :, col + n * DH : col + (n + 1) * DH] = (
                    dq[:, n * DH : (n + 1) * DH].T * SCALE
                ).astype(bf16)
        dks_v[slot] = (dk * SCALE).astype(bf16)
        dvs_v[slot] = dv.astype(bf16)

    score_item(c, c >= 0)
    score_item(late_own, c >= 0)

    for late in (0, 1):
        j = chunk_of(1, late, z)

        @pl.when(arrives(late))
        def _():
            ag_copy(j, 2, across).wait_recv()
            for way in (0, 1):

                @pl.when(hops(way, 1, late, z) >= 1)
                def _():
                    ag_copy(j, way, beside[way]).start()

    def foreign_score(late, carry):
        score_item(chunk_of(1, late, z), arrives(late))
        return carry

    lax.fori_loop(0, 2, foreign_score, 0)

    for copy in short_loads:
        copy.wait()

    def score_across(step):
        def item(n, carry):
            late, way = n // 2, lax.rem(n, 2)
            j = chunk_of(1, late, root_of(way, step))

            @pl.when(comes_across(late, way, step))
            def _():
                ag_copy(j, 2, across).wait_recv()
                score_item(j, c >= 0)

            return carry

        @pl.when(step >= 1)
        def _():
            lax.fori_loop(0, 4, item, 0)

    def gather_step(step, carry):
        for foreign in (0, 1):
            for late in (0, 1):
                for way in (0, 1):
                    z_root = root_of(way, step)
                    j = chunk_of(foreign, late, z_root)
                    reach = hops(way, foreign, late, z_root)

                    @pl.when(reach >= step)
                    def _():
                        ag_copy(j, way, beside[way]).wait_recv()

                    @pl.when(reach >= step + 1)
                    def _():
                        ag_copy(j, way, beside[way]).start()

                    if foreign == 0:

                        @pl.when(goes_across(late, way, step))
                        def _():
                            ag_copy(j, 2, across).start()

        @pl.when(step <= SLOTS)
        def _():
            short_slot(step - 1)

        def item(n, carry):
            foreign, late, way = n // 4, lax.rem(n // 2, 2), lax.rem(n, 2)
            z_root = root_of(way, step)
            score_item(chunk_of(foreign, late, z_root), hops(way, foreign, late, z_root) >= step)
            return carry

        lax.fori_loop(0, 8, item, carry)
        score_across(step - 1)
        return carry

    lax.fori_loop(1, LAST_STEP + 2, gather_step, 0)

    short_stores = [
        pltpu.make_async_copy(src, dst.at[0], out_sem.at[n])
        for n, (src, dst) in enumerate(((dqs_v, dqs_hbm), (dks_v, dks_hbm), (dvs_v, dvs_hbm)))
    ]
    for copy in short_stores:
        copy.start()

    for half in (0, 1):
        m = jnp.max(m_v[half], axis=0, keepdims=True)
        lse_v[half] = m + jnp.log2(jnp.sum(l_v[half] * jnp.exp2(m_v[half] - m), axis=0, keepdims=True))

    def grad_tiles(which, j):
        values = kv[j, 1]
        p_parts, ds_parts, q_parts, do_parts = [], [], [], []
        for half in which:
            rows, own_chunk = halves[half]
            slot = slot_of(half, j)
            for col in PAIRS:
                cols = slice(col, col + 2 * DH)
                grads = heads(do_v.at[rows], col)
                p = jnp.exp2(scores[slot, :, cols] - lse_v[half, :, cols])
                ds = (p * (nt(values, grads) - delta_v[half, :, cols])).astype(bf16)
                ds_v[slot, :, cols] = ds
                p_parts.append(p.astype(bf16))
                ds_parts.append(ds)
                q_parts.append(heads(q_v.at[rows], col))
                do_parts.append(grads)
        acc[0] = nn(jnp.concatenate(ds_parts, axis=1), jnp.concatenate(q_parts, axis=0))
        acc[1] = nn(jnp.concatenate(p_parts, axis=1), jnp.concatenate(do_parts, axis=0))

    def grad_item(j):
        @pl.when(~(early_needs(j) | late_needs(j)))
        def _():
            acc[...] = jnp.zeros((2, CH, DH), f32)

        for_needed(j, c >= 0, grad_tiles)

    def grads_across(step):
        def item(n, carry):
            late, way = n // 2, lax.rem(n, 2)
            j = chunk_of(1, late, root_of(way, step))

            @pl.when(comes_across(late, way, step))
            def _():
                grad_item(j)
                snd[j] = acc[...].astype(bf16)
                rs_copy(j, 2, across).start()

            return carry

        @pl.when(step >= 1)
        def _():
            lax.fori_loop(0, 4, item, 0)

    def add_term(way, j, target):
        rs_copy(j, way, target).wait_recv()
        acc[...] += rcv[way, j].astype(f32)

    def scatter_step(back, carry):
        step = LAST_STEP + 1 - back
        grads_across(step - 1)

        def item(n, carry):
            foreign, late, way = n // 4, lax.rem(n // 2, 2), lax.rem(n, 2)
            z_root = root_of(way, step)
            j = chunk_of(foreign, late, z_root)
            reach = hops(way, foreign, late, z_root)

            @pl.when(reach >= step)
            def _():
                grad_item(j)

                @pl.when(reach >= step + 1)
                def _():
                    add_term(way, j, beside[0])

                @pl.when((foreign == 0) & goes_across(late, way, step))
                def _():
                    add_term(2, j, across)

                snd[j] = acc[...].astype(bf16)
                rs_copy(j, way, choose(way, beside[0], beside[1])).start()

            return carry

        return lax.fori_loop(0, 8, item, carry)

    lax.fori_loop(0, LAST_STEP + 1, scatter_step, 0)

    def collect(foreign, late, j):
        for way in (0, 1):

            @pl.when(hops(way, foreign, late, z) >= 1)
            def _():
                add_term(way, j, beside[way])

    def foreign_root(late, carry):
        j = chunk_of(1, late, z)

        @pl.when(arrives(late))
        def _():
            grad_item(j)
            collect(1, late, j)
            snd[j] = acc[...].astype(bf16)
            rs_copy(j, 2, across).start()

        return carry

    lax.fori_loop(0, 2, foreign_root, 0)

    def own_root(late, carry):
        grad_item(chunk_of(0, late, z))
        own[late] = acc[...]
        return carry

    lax.fori_loop(0, 2, own_root, 0)

    def tn(a, b):
        return lax.dot_general(a, b, (((0,), (0,)), ((), ())), preferred_element_type=f32)

    def dq_early(first, count):
        keys = kv[pl.ds(first, count), 0].reshape(count * CH, DH)
        for col in PAIRS:
            cols = slice(col, col + 2 * DH)
            dqt[0, :, cols] += tn(keys, ds_v[pl.ds(first, count), :, cols].reshape(count * CH, 2 * DH))

    def dq_early_two(n, carry):
        dq_early(2 * n, 2)
        return carry

    lax.fori_loop(0, (c + 1) // 2, dq_early_two, 0)

    @pl.when(lax.rem(c, 2) == 0)
    def _():
        dq_early(c, 1)

    keys = kv[pl.ds(15 - c, 17), 0].reshape(17 * CH, DH)
    for col in PAIRS:
        cols = slice(col, col + 2 * DH)
        dqt[1, :, cols] = tn(keys, ds_v[NCTX : NCTX + 17, :, cols].reshape(17 * CH, 2 * DH))
    for half, (rows, own_chunk) in enumerate(halves):
        for col in range(0, HC, DH):
            dq_v[rows, col : col + DH] = (dqt[half, :, col : col + DH].T * SCALE).astype(bf16)
    dq_store = pltpu.make_async_copy(dq_v, dq_hbm.at[0], out_sem.at[3])
    dq_store.start()

    def own_total(late, carry):
        acc[...] = own[late]
        j = chunk_of(0, late, z)
        collect(0, late, j)

        @pl.when(crosses(late))
        def _():
            add_term(2, j, across)

        rows = pl.ds(pl.multiple_of(late * CH, CH), CH)
        dkv_v[0, rows] = (acc[0] * SCALE).astype(bf16)
        dkv_v[1, rows] = acc[1].astype(bf16)
        return carry

    lax.fori_loop(0, 2, own_total, 0)
    kv_stores = [
        pltpu.make_async_copy(dkv_v.at[n], dst.at[0], out_sem.at[4 + n]) for n, dst in enumerate((dk_hbm, dv_hbm))
    ]
    for copy in kv_stores:
        copy.start()

    for late in (0, 1):
        j = chunk_of(0, late, z)

        @pl.when(crosses(late))
        def _():
            ag_copy(j, 2, across).wait_send()

        for foreign in (0, 1):
            j = chunk_of(foreign, late, z)
            for way in (0, 1):

                @pl.when(hops(way, foreign, late, z) >= 1)
                def _():
                    ag_copy(j, way, beside[way]).wait_send()

        @pl.when(arrives(late))
        def _():
            rs_copy(chunk_of(1, late, z), 2, across).wait_send()

    def sent_step(step, carry):
        def item(n, carry):
            foreign, late, way = n // 4, lax.rem(n // 2, 2), lax.rem(n, 2)
            z_root = root_of(way, step)
            j = chunk_of(foreign, late, z_root)
            reach = hops(way, foreign, late, z_root)

            @pl.when(reach >= step)
            def _():
                rs_copy(j, way, beside[0]).wait_send()

            @pl.when(reach >= step + 1)
            def _():
                ag_copy(j, way, beside[0]).wait_send()

            @pl.when((foreign == 0) & goes_across(late, way, step))
            def _():
                ag_copy(j, 2, across).wait_send()

            @pl.when((foreign == 1) & comes_across(late, way, step))
            def _():
                rs_copy(j, 2, across).wait_send()

            return carry

        return lax.fori_loop(0, 8, item, carry)

    lax.fori_loop(1, LAST_STEP + 1, sent_step, 0)

    for copy in short_stores + [dq_store] + kv_stores:
        copy.wait()


def emit(*refs):
    ins, outs, held, in_sem, out_sem = refs[:6], refs[6:12], refs[12:18], refs[18], refs[19]
    loads = [pltpu.make_async_copy(ins[n], held[n], in_sem.at[n]) for n in range(6)]
    stores = [pltpu.make_async_copy(held[n], outs[n], out_sem.at[n]) for n in range(6)]
    for load in loads:
        load.start()
    for load, store in zip(loads, stores):
        load.wait()
        store.start()
    for store in stores:
        store.wait()


def body(*args):
    bf16, f32 = jnp.bfloat16, jnp.float32
    tok = args[0].shape[1]
    any_spec = pl.BlockSpec(memory_space=pltpu.HBM)
    smem_spec = pl.BlockSpec(memory_space=pltpu.SMEM)
    in_specs = [any_spec] * 5 + [smem_spec] + [any_spec] * 5 + [smem_spec] * 2
    out_shape = [jax.ShapeDtypeStruct(args[n].shape, bf16) for n in (0, 1, 2, 6, 7, 8)]
    dma = pltpu.SemaphoreType.DMA
    scratch = [
        pltpu.VMEM((NCHUNK, 2, CH, DH), bf16),
        pltpu.VMEM((tok, HC), bf16),
        pltpu.VMEM((tok, HC), bf16),
        pltpu.VMEM((tok, HC), bf16),
        pltpu.VMEM((33, CH, HC), f32),
        pltpu.VMEM((33, CH, HC), bf16),
        pltpu.VMEM((2, 8, HC), f32),
        pltpu.VMEM((2, 8, HC), f32),
        pltpu.VMEM((2, 1, HC), f32),
        pltpu.VMEM((2, 1, HC), f32),
        pltpu.VMEM((2, 1, 2 * DH), jnp.int32),
        pltpu.VMEM((2, DH, HC), f32),
        pltpu.VMEM((2, CH, DH), f32),
        pltpu.VMEM((2, 2, CH, DH), f32),
        pltpu.VMEM((NCHUNK, 2, CH, DH), bf16),
        pltpu.VMEM((3, NCHUNK, 2, CH, DH), bf16),
        pltpu.VMEM((SLOTS, CH, HC), bf16),
        pltpu.VMEM((SLOTS, CH, DH), bf16),
        pltpu.VMEM((SLOTS, CH, DH), bf16),
        pltpu.VMEM((SLOTS, CH, HC), bf16),
        pltpu.VMEM((SLOTS, CH, HC), bf16),
        pltpu.VMEM((tok, HC), bf16),
        pltpu.VMEM((2, tok, DH), bf16),
        pltpu.VMEM((SLOTS, CH, HC), bf16),
        pltpu.VMEM((SLOTS, CH, DH), bf16),
        pltpu.VMEM((SLOTS, CH, DH), bf16),
        dma((12,)),
        dma((6,)),
        dma((NCHUNK, 3)),
        dma((NCHUNK,)),
        dma((NCHUNK,)),
        dma((3, NCHUNK)),
    ]
    grads = pl.pallas_call(
        kernel,
        out_shape=out_shape,
        in_specs=in_specs,
        out_specs=[any_spec] * 6,
        scratch_shapes=scratch,
        compiler_params=pltpu.CompilerParams(
            collective_id=0, has_side_effects=True, vmem_limit_bytes=60 * 1024 * 1024
        ),
        name="attention_backward",
    )(*args)
    return tuple(
        pl.pallas_call(
            emit,
            out_shape=out_shape,
            in_specs=[any_spec] * 6,
            out_specs=[any_spec] * 6,
            scratch_shapes=[pltpu.VMEM(out.shape, bf16) for out in out_shape] + [dma((6,)), dma((6,))],
            compiler_params=pltpu.CompilerParams(vmem_limit_bytes=60 * 1024 * 1024),
            name="emit",
        )(*grads)
    )


def solution(mesh):
    seq = P("dp", "ctx", None)
    slot = P("dp", "ctx", None, None)
    return jax.shard_map(
        body,
        mesh=mesh,
        in_specs=(seq,) * 5 + (P("dp", None),) + (slot,) * 5 + (P("dp", "ctx"),) * 2,
        out_specs=(seq, seq, seq, slot, slot, slot),
        check_vma=False,
    )
```

```python
import math

import jax
import jax.numpy as jnp
from jax import lax
from jax.experimental import pallas as pl
from jax.experimental.pallas import tpu as pltpu
from jax.sharding import PartitionSpec as P

H = 6
DH = 128
CH = 128
NZ = 8
NCTX = 16
NCHUNK = 32
NDOC = 4
SLOTS = 4
HC = H * DH
PAIRS = tuple(range(0, HC, 2 * DH))
SCALE = 1.0 / math.sqrt(DH)
SCALE2 = SCALE * math.log2(math.e)
NEG = -1e30
LAST_STEP = 4

HOPS_UP = {
    (0, 0, 0): (3, 3, 3, 4, 3, 2, 1, 0),
    (0, 0, 1): (0, 0, 0, 0, 0, 4, 4, 4),
    (0, 1, 0): (0, 0, 3, 4, 3, 2, 4, 4),
    (0, 1, 1): (4, 3, 4, 3, 4, 3, 4, 3),
    (1, 0, 0): (4, 4, 4, 4, 4, 4, 4, 4),
    (1, 0, 1): (0, 0, 0, 0, 0, 4, 4, 4),
    (1, 1, 0): (4, 3, 4, 3, 4, 3, 4, 3),
    (1, 1, 1): (0, 0, 0, 0, 0, 0, 0, 0),
}
HOPS_DOWN = {
    (0, 0, 0): (4, 4, 4, 0, 0, 0, 0, 0),
    (0, 0, 1): (0, 1, 2, 3, 4, 3, 3, 3),
    (0, 1, 0): (1, 3, 4, 0, 1, 3, 3, 3),
    (0, 1, 1): (3, 4, 3, 4, 3, 4, 3, 4),
    (1, 0, 0): (3, 3, 3, 3, 3, 3, 3, 3),
    (1, 0, 1): (0, 1, 2, 3, 4, 3, 3, 3),
    (1, 1, 0): (3, 4, 3, 4, 3, 4, 3, 4),
    (1, 1, 1): (0, 0, 0, 0, 0, 0, 0, 0),
}


def needed(j, c):
    return j <= c or 15 - c <= j <= 31 - c


def device_masks(c):
    x, z = divmod(c, NZ)
    across = (1 - x) * NZ + z
    hops = (HOPS_UP, HOPS_DOWN)

    def chunk(plane, late, zr):
        owner = plane * NZ + zr
        return 2 * NCTX - 1 - owner if late else owner

    def over_x(plane, late, way, step, to):
        zr = (z + step if way else z - step) % NZ
        near, far = hops[way][1 - plane, 1, late][zr], hops[1 - way][1 - plane, 1, late][zr]
        there = hops[way][plane, 0, late][zr]
        return there >= step and near < step and far < NZ - step and needed(chunk(plane, late, zr), to)

    def root_over_x(plane, late, to):
        on = hops[0][1 - plane, 1, late][z] + hops[1][1 - plane, 1, late][z]
        return on >= 1 or needed(chunk(plane, late, z), to)

    has = forwards = over = root = 0
    for late in (0, 1):
        root |= root_over_x(x, late, across) << late
        root |= root_over_x(1 - x, late, c) << (2 + late)
        for way in (0, 1):
            for foreign in (0, 1):
                n = 4 * foreign + 2 * late + way
                root |= (hops[way][x, foreign, late][z] >= 1) << (4 + n)
                for step in range(1, LAST_STEP + 1):
                    zr = (z + step if way else z - step) % NZ
                    reach = hops[way][x, foreign, late][zr]
                    has |= (reach >= step) << (8 * (step - 1) + n)
                    forwards |= (reach >= step + 1) << (8 * (step - 1) + n)
            for step in range(1, LAST_STEP + 1):
                bit = 4 * (step - 1) + 2 * late + way
                over |= over_x(x, late, way, step, across) << bit
                over |= over_x(1 - x, late, way, step, c) << (16 + bit)
    return tuple(m - (1 << 32) if m >= 1 << 31 else m for m in (has, forwards, over, root))


def nt(a, b):
    return lax.dot_general(a, b, (((1,), (1,)), ((), ())), preferred_element_type=jnp.float32)


def nn(a, b):
    return lax.dot_general(a, b, (((1,), (0,)), ((), ())), preferred_element_type=jnp.float32)


def heads(ref, col):
    return jnp.concatenate([ref[:, col : col + DH], ref[:, col + DH : col + 2 * DH]], axis=0)


def row_delta(grads, outs):
    prod = grads.astype(jnp.float32) * outs.astype(jnp.float32)
    high = prod.astype(jnp.bfloat16)
    low = (prod - high.astype(jnp.float32)).astype(jnp.bfloat16)
    ones = jnp.ones((16, DH), jnp.bfloat16)
    return (nt(ones, high) + nt(ones, low))[0:1]


def kernel(
    q_hbm, k_hbm, v_hbm, o_hbm, do_hbm, doc_ref,
    qs_hbm, ks_hbm, vs_hbm, os_hbm, dos_hbm, slen_ref, scount_ref,
    dq_hbm, dk_hbm, dv_hbm, dqs_hbm, dks_hbm, dvs_hbm,
    kv, q_v, o_v, do_v, qt_v, dot_v, scores, ds_v, m_v, l_v, lse_v, delta_v, lo_v, dqt, acc, own,
    snd, rcv, qs_v, ks_v, vs_v, os_v, dos_v, dq_v, dkv_v, dqs_v, dks_v, dvs_v,
    in_sem, out_sem, ag_send, ag_recv, rs_send, rs_recv,
):
    f32, bf16 = jnp.float32, jnp.bfloat16
    c = lax.axis_index("ctx")
    x = c // NZ
    z = c - x * NZ
    late_own = 2 * NCTX - 1 - c
    z_up = lax.rem(z + 1, NZ)
    z_down = lax.rem(z + NZ - 1, NZ)
    across = (1 - x) * NZ + z
    beside = (x * NZ + z_up, x * NZ + z_down)

    masks = [jnp.int32(m) for m in device_masks(0)]
    for device in range(1, NCTX):
        here = c == device
        masks = [jnp.where(here, jnp.int32(m), old) for m, old in zip(device_masks(device), masks)]
    has_mask, forward_mask, over_mask, root_mask = masks

    def bit(mask, n):
        return ((mask >> n) & 1) == 1

    def has(step, n):
        return bit(has_mask, 8 * (step - 1) + n)

    def forwards(step, n):
        return bit(forward_mask, 8 * (step - 1) + n)

    def goes_across(step, n):
        return bit(over_mask, 4 * (step - 1) + n)

    def comes_across(step, n):
        return bit(over_mask, 16 + 4 * (step - 1) + n)

    def crosses(late):
        return bit(root_mask, late)

    def arrives(late):
        return bit(root_mask, 2 + late)

    def sets_out(foreign, late, way):
        return bit(root_mask, 4 + 4 * foreign + 2 * late + way)

    def choose(flag, one, zero):
        if isinstance(flag, int):
            return one if flag else zero
        return jnp.where(flag == 1, one, zero)

    def chunk_of(foreign, late, z_root):
        owner = (x + foreign * (1 - 2 * x)) * NZ + z_root
        return owner + late * (2 * NCTX - 1 - 2 * owner)

    def root_of(way, step):
        return (z + NZ + step * (2 * way - 1)) & (NZ - 1)

    def early_needs(j, who=c):
        return j <= who

    def late_needs(j, who=c):
        return (j >= 15 - who) & (j <= 2 * NCTX - 1 - who)

    def ag_copy(j, way, target):
        return pltpu.make_async_remote_copy(
            src_ref=kv.at[j], dst_ref=kv.at[j], send_sem=ag_send.at[j, way], recv_sem=ag_recv.at[j],
            device_id={"ctx": target}, device_id_type=pl.DeviceIdType.MESH,
        )

    def rs_copy(j, way, target):
        return pltpu.make_async_remote_copy(
            src_ref=snd.at[j], dst_ref=rcv.at[way, j], send_sem=rs_send.at[j], recv_sem=rs_recv.at[way, j],
            device_id={"ctx": target}, device_id_type=pl.DeviceIdType.MESH,
        )

    kv_loads = [
        pltpu.make_async_copy(src.at[0, pl.ds(half * CH, CH)], kv.at[j, which], in_sem.at[2 * which + half])
        for which, src in ((0, k_hbm), (1, v_hbm))
        for half, j in ((0, c), (1, late_own))
    ]
    long_loads = [
        pltpu.make_async_copy(src.at[0], dst, in_sem.at[4 + n])
        for n, (src, dst) in enumerate(((q_hbm, q_v), (do_hbm, do_v), (o_hbm, o_v)))
    ]
    short_loads = [
        pltpu.make_async_copy(src.at[0], dst, in_sem.at[7 + n])
        for n, (src, dst) in enumerate(
            ((qs_hbm, qs_v), (ks_hbm, ks_v), (vs_hbm, vs_v), (os_hbm, os_v), (dos_hbm, dos_v))
        )
    ]
    for copy in kv_loads + long_loads + short_loads:
        copy.start()

    barrier = pltpu.get_barrier_semaphore()
    for target in beside + (across,):
        pl.semaphore_signal(
            barrier, inc=1, device_id={"ctx": target}, device_id_type=pl.DeviceIdType.MESH
        )
    pl.semaphore_wait(barrier, 3)

    for copy in kv_loads:
        copy.wait()
    for late in (0, 1):
        j = chunk_of(0, late, z)

        @pl.when(crosses(late))
        def _():
            ag_copy(j, 2, across).start()

    for late in (0, 1):
        j = chunk_of(0, late, z)
        for way in (0, 1):

            @pl.when(sets_out(0, late, way))
            def _():
                ag_copy(j, way, beside[way]).start()

    for copy in long_loads:
        copy.wait()
    halves = [(pl.ds(half * CH, CH), own_chunk) for half, own_chunk in ((0, c), (1, late_own))]
    ends = []
    total = doc_ref[0, 0]
    for d in range(NDOC):
        ends.append(total)
        if d + 1 < NDOC:
            total = total + doc_ref[0, d + 1]
    lane = lax.rem(lax.broadcasted_iota(jnp.int32, (1, 2 * DH), 1), CH)
    sub = lax.broadcasted_iota(jnp.int32, (CH, 1), 0)
    for half, (rows, own_chunk) in enumerate(halves):
        pos = own_chunk * CH + lane
        first = jnp.zeros((1, 2 * DH), jnp.int32)
        for end in ends:
            first = jnp.maximum(first, jnp.where(pos >= end, end, 0))
        lo_v[half] = first
        for col in PAIRS:
            delta_v[half, :, col : col + 2 * DH] = row_delta(heads(do_v.at[rows], col), heads(o_v.at[rows], col))
        for col in range(0, HC, DH):
            qt_v[half, :, col : col + DH] = q_v[rows, col : col + DH].T
            dot_v[half, :, col : col + DH] = do_v[rows, col : col + DH].T
        m_v[half] = jnp.full((8, HC), NEG, f32)
        l_v[half] = jnp.zeros((8, HC), f32)
    dqt[0] = jnp.zeros((DH, HC), f32)

    def slot_of(half, j):
        return j if half == 0 else NCTX + j - (15 - c)

    def score_tiles(which, j):
        keys = kv[j, 0]
        key_pos = j * CH + sub
        for half in which:
            own_chunk = halves[half][1]
            visible = (key_pos >= lo_v[half]) & (key_pos <= own_chunk * CH + lane)
            bias = jnp.where(visible, 0.0, NEG)
            slot = slot_of(half, j)
            for col in PAIRS:
                cols = slice(col, col + 2 * DH)
                s = nn(keys, qt_v[half, :, cols]) * SCALE2 + bias
                scores[slot, :, cols] = s
                s = s.reshape(CH // 8, 8, 2 * DH)
                m_old = m_v[half, :, cols]
                m_new = jnp.maximum(m_old, jnp.max(s, axis=0))
                m_v[half, :, cols] = m_new
                l_v[half, :, cols] = l_v[half, :, cols] * jnp.exp2(m_old - m_new) + jnp.sum(
                    jnp.exp2(s - m_new[None]), axis=0
                )

    def for_needed(j, has, tiles):
        early, late = early_needs(j), late_needs(j)
        for which, wanted in (((0, 1), early & late), ((0,), early & ~late), ((1,), late & ~early)):

            @pl.when(has & wanted)
            def _():
                tiles(which, j)

    def score_item(j, has):
        for_needed(j, has, score_tiles)

    def short_slot(slot):
        length = jnp.where(slot < scount_ref[0, 0], slen_ref[0, slot], 0)
        keys = ks_v[slot]
        values = vs_v[slot]
        visible = (sub <= lane) & (lane < length)
        dk = jnp.zeros((CH, DH), f32)
        dv = jnp.zeros((CH, DH), f32)
        for col in PAIRS:
            queries = heads(qs_v.at[slot], col)
            grads = heads(dos_v.at[slot], col)
            delta = row_delta(grads, heads(os_v.at[slot], col))
            s = jnp.where(visible, nt(keys, queries) * SCALE2, NEG)
            e = jnp.exp2(s - jnp.max(s, axis=0, keepdims=True))
            inverse = jnp.where(lane < length, 1.0 / jnp.sum(e, axis=0, keepdims=True), 0.0)
            p = e * inverse
            ds = (p * (nt(values, grads) - delta)).astype(bf16)
            dv = dv + nn(p.astype(bf16), grads)
            dk = dk + nn(ds, queries)
            dq = lax.dot_general(keys, ds, (((0,), (0,)), ((), ())), preferred_element_type=f32)
            for n in (0, 1):
                dqs_v[slot, :, col + n * DH : col + (n + 1) * DH] = (
                    dq[:, n * DH : (n + 1) * DH].T * SCALE
                ).astype(bf16)
        dks_v[slot] = (dk * SCALE).astype(bf16)
        dvs_v[slot] = dv.astype(bf16)

    score_item(c, c >= 0)
    score_item(late_own, c >= 0)

    for late in (0, 1):
        j = chunk_of(1, late, z)

        @pl.when(arrives(late))
        def _():
            ag_copy(j, 2, across).wait_recv()
            for way in (0, 1):

                @pl.when(sets_out(1, late, way))
                def _():
                    ag_copy(j, way, beside[way]).start()

    def foreign_score(late, carry):
        score_item(chunk_of(1, late, z), arrives(late))
        return carry

    lax.fori_loop(0, 2, foreign_score, 0)

    for copy in short_loads:
        copy.wait()

    def score_across(step):
        def item(n, carry):
            j = chunk_of(1, n // 2, root_of(lax.rem(n, 2), step))

            @pl.when(comes_across(step, n))
            def _():
                ag_copy(j, 2, across).wait_recv()
                score_item(j, c >= 0)

            return carry

        @pl.when(step >= 1)
        def _():
            lax.fori_loop(0, 4, item, 0)

    def gather_step(step, carry):
        for n in range(8):
            foreign, late, way = n // 4, n // 2 % 2, n % 2
            j = chunk_of(foreign, late, root_of(way, step))

            @pl.when(has(step, n))
            def _():
                ag_copy(j, way, beside[way]).wait_recv()

            @pl.when(forwards(step, n))
            def _():
                ag_copy(j, way, beside[way]).start()

            if foreign == 0:

                @pl.when(goes_across(step, n))
                def _():
                    ag_copy(j, 2, across).start()

        short_slot(step - 1)

        def item(n, carry):
            foreign, late, way = n // 4, (n // 2) & 1, n & 1
            score_item(chunk_of(foreign, late, root_of(way, step)), has(step, n))
            return carry

        lax.fori_loop(0, 8, item, carry)
        score_across(step - 1)
        return carry

    lax.fori_loop(1, LAST_STEP + 1, gather_step, 0)
    score_across(LAST_STEP)

    short_stores = [
        pltpu.make_async_copy(src, dst.at[0], out_sem.at[n])
        for n, (src, dst) in enumerate(((dqs_v, dqs_hbm), (dks_v, dks_hbm), (dvs_v, dvs_hbm)))
    ]
    for copy in short_stores:
        copy.start()

    for half in (0, 1):
        m = jnp.max(m_v[half], axis=0, keepdims=True)
        lse_v[half] = m + jnp.log2(jnp.sum(l_v[half] * jnp.exp2(m_v[half] - m), axis=0, keepdims=True))

    def grad_tiles(which, j):
        values = kv[j, 1]
        p_parts, ds_parts, q_parts, do_parts = [], [], [], []
        for half in which:
            rows, own_chunk = halves[half]
            slot = slot_of(half, j)
            for col in PAIRS:
                cols = slice(col, col + 2 * DH)
                grads = heads(do_v.at[rows], col)
                p = jnp.exp2(scores[slot, :, cols] - lse_v[half, :, cols])
                ds = (p * (nn(values, dot_v[half, :, cols]) - delta_v[half, :, cols])).astype(bf16)
                ds_v[slot, :, cols] = ds
                p_parts.append(p.astype(bf16))
                ds_parts.append(ds)
                q_parts.append(heads(q_v.at[rows], col))
                do_parts.append(grads)
        acc[0] = nn(jnp.concatenate(ds_parts, axis=1), jnp.concatenate(q_parts, axis=0))
        acc[1] = nn(jnp.concatenate(p_parts, axis=1), jnp.concatenate(do_parts, axis=0))

    def grad_item(j):
        @pl.when(~(early_needs(j) | late_needs(j)))
        def _():
            acc[...] = jnp.zeros((2, CH, DH), f32)

        for_needed(j, c >= 0, grad_tiles)

    def grads_across(step):
        def item(n, carry):
            j = chunk_of(1, n // 2, root_of(lax.rem(n, 2), step))

            @pl.when(comes_across(step, n))
            def _():
                grad_item(j)
                snd[j] = acc[...].astype(bf16)
                rs_copy(j, 2, across).start()

            return carry

        @pl.when(step >= 1)
        def _():
            lax.fori_loop(0, 4, item, 0)

    def add_term(way, j, target):
        rs_copy(j, way, target).wait_recv()
        acc[...] += rcv[way, j].astype(f32)

    def scatter_step(back, carry):
        step = LAST_STEP - back
        grads_across(step - 1)

        def item(n, carry):
            foreign, late, way = n // 4, (n // 2) & 1, n & 1
            j = chunk_of(foreign, late, root_of(way, step))

            @pl.when(has(step, n))
            def _():
                grad_item(j)

                @pl.when(forwards(step, n))
                def _():
                    add_term(way, j, beside[0])

                @pl.when((foreign == 0) & goes_across(step, n & 3))
                def _():
                    add_term(2, j, across)

                snd[j] = acc[...].astype(bf16)
                rs_copy(j, way, choose(way, beside[0], beside[1])).start()

            return carry

        return lax.fori_loop(0, 8, item, carry)

    grads_across(LAST_STEP)
    lax.fori_loop(0, LAST_STEP, scatter_step, 0)

    def collect(foreign, late, j):
        for way in (0, 1):

            @pl.when(sets_out(foreign, late, way))
            def _():
                add_term(way, j, beside[way])

    def foreign_root(late, carry):
        j = chunk_of(1, late, z)

        @pl.when(arrives(late))
        def _():
            grad_item(j)
            collect(1, late, j)
            snd[j] = acc[...].astype(bf16)
            rs_copy(j, 2, across).start()

        return carry

    lax.fori_loop(0, 2, foreign_root, 0)

    def own_root(late, carry):
        grad_item(chunk_of(0, late, z))
        own[late] = acc[...]
        return carry

    lax.fori_loop(0, 2, own_root, 0)

    def tn(a, b):
        return lax.dot_general(a, b, (((0,), (0,)), ((), ())), preferred_element_type=f32)

    def dq_early(first, count):
        keys = kv[pl.ds(first, count), 0].reshape(count * CH, DH)
        for col in PAIRS:
            cols = slice(col, col + 2 * DH)
            dqt[0, :, cols] += tn(keys, ds_v[pl.ds(first, count), :, cols].reshape(count * CH, 2 * DH))

    def dq_early_two(n, carry):
        dq_early(2 * n, 2)
        return carry

    lax.fori_loop(0, (c + 1) // 2, dq_early_two, 0)

    @pl.when(lax.rem(c, 2) == 0)
    def _():
        dq_early(c, 1)

    keys = kv[pl.ds(15 - c, 17), 0].reshape(17 * CH, DH)
    for col in PAIRS:
        cols = slice(col, col + 2 * DH)
        dqt[1, :, cols] = tn(keys, ds_v[NCTX : NCTX + 17, :, cols].reshape(17 * CH, 2 * DH))
    for half, (rows, own_chunk) in enumerate(halves):
        for col in range(0, HC, DH):
            dq_v[rows, col : col + DH] = (dqt[half, :, col : col + DH].T * SCALE).astype(bf16)
    dq_store = pltpu.make_async_copy(dq_v, dq_hbm.at[0], out_sem.at[3])
    dq_store.start()

    for late in (0, 1):
        j = chunk_of(0, late, z)

        @pl.when(crosses(late))
        def _():
            ag_copy(j, 2, across).wait_send()

        for foreign in (0, 1):
            j = chunk_of(foreign, late, z)
            for way in (0, 1):

                @pl.when(sets_out(foreign, late, way))
                def _():
                    ag_copy(j, way, beside[way]).wait_send()

        @pl.when(arrives(late))
        def _():
            rs_copy(chunk_of(1, late, z), 2, across).wait_send()

    def sent_step(step, carry):
        for n in range(8):
            foreign, late, way = n // 4, n // 2 % 2, n % 2
            j = chunk_of(foreign, late, root_of(way, step))

            @pl.when(has(step, n))
            def _():
                rs_copy(j, way, beside[0]).wait_send()

            @pl.when(forwards(step, n))
            def _():
                ag_copy(j, way, beside[0]).wait_send()

            if foreign == 0:

                @pl.when(goes_across(step, n))
                def _():
                    ag_copy(j, 2, across).wait_send()

            else:

                @pl.when(comes_across(step, n & 3))
                def _():
                    rs_copy(j, 2, across).wait_send()

        return carry

    lax.fori_loop(1, LAST_STEP + 1, sent_step, 0)

    def own_total(late, carry):
        acc[...] = own[late]
        j = chunk_of(0, late, z)
        collect(0, late, j)

        @pl.when(crosses(late))
        def _():
            add_term(2, j, across)

        rows = pl.ds(pl.multiple_of(late * CH, CH), CH)
        dkv_v[0, rows] = (acc[0] * SCALE).astype(bf16)
        dkv_v[1, rows] = acc[1].astype(bf16)
        return carry

    lax.fori_loop(0, 2, own_total, 0)
    kv_stores = [
        pltpu.make_async_copy(dkv_v.at[n], dst.at[0], out_sem.at[4 + n]) for n, dst in enumerate((dk_hbm, dv_hbm))
    ]
    for copy in kv_stores:
        copy.start()

    for copy in short_stores + [dq_store] + kv_stores:
        copy.wait()


def emit(*refs):
    ins, outs, held, in_sem, out_sem = refs[:6], refs[6:12], refs[12:18], refs[18], refs[19]
    loads = [pltpu.make_async_copy(ins[n], held[n], in_sem.at[n]) for n in range(6)]
    stores = [pltpu.make_async_copy(held[n], outs[n], out_sem.at[n]) for n in range(6)]
    for load in loads:
        load.start()
    for load, store in zip(loads, stores):
        load.wait()
        store.start()
    for store in stores:
        store.wait()


def body(*args):
    bf16, f32 = jnp.bfloat16, jnp.float32
    tok = args[0].shape[1]
    any_spec = pl.BlockSpec(memory_space=pltpu.HBM)
    smem_spec = pl.BlockSpec(memory_space=pltpu.SMEM)
    in_specs = [any_spec] * 5 + [smem_spec] + [any_spec] * 5 + [smem_spec] * 2
    out_shape = [jax.ShapeDtypeStruct(args[n].shape, bf16) for n in (0, 1, 2, 6, 7, 8)]
    dma = pltpu.SemaphoreType.DMA
    scratch = [
        pltpu.VMEM((NCHUNK, 2, CH, DH), bf16),
        pltpu.VMEM((tok, HC), bf16),
        pltpu.VMEM((tok, HC), bf16),
        pltpu.VMEM((tok, HC), bf16),
        pltpu.VMEM((2, DH, HC), bf16),
        pltpu.VMEM((2, DH, HC), bf16),
        pltpu.VMEM((33, CH, HC), f32),
        pltpu.VMEM((33, CH, HC), bf16),
        pltpu.VMEM((2, 8, HC), f32),
        pltpu.VMEM((2, 8, HC), f32),
        pltpu.VMEM((2, 1, HC), f32),
        pltpu.VMEM((2, 1, HC), f32),
        pltpu.VMEM((2, 1, 2 * DH), jnp.int32),
        pltpu.VMEM((2, DH, HC), f32),
        pltpu.VMEM((2, CH, DH), f32),
        pltpu.VMEM((2, 2, CH, DH), f32),
        pltpu.VMEM((NCHUNK, 2, CH, DH), bf16),
        pltpu.VMEM((3, NCHUNK, 2, CH, DH), bf16),
        pltpu.VMEM((SLOTS, CH, HC), bf16),
        pltpu.VMEM((SLOTS, CH, DH), bf16),
        pltpu.VMEM((SLOTS, CH, DH), bf16),
        pltpu.VMEM((SLOTS, CH, HC), bf16),
        pltpu.VMEM((SLOTS, CH, HC), bf16),
        pltpu.VMEM((tok, HC), bf16),
        pltpu.VMEM((2, tok, DH), bf16),
        pltpu.VMEM((SLOTS, CH, HC), bf16),
        pltpu.VMEM((SLOTS, CH, DH), bf16),
        pltpu.VMEM((SLOTS, CH, DH), bf16),
        dma((12,)),
        dma((6,)),
        dma((NCHUNK, 3)),
        dma((NCHUNK,)),
        dma((NCHUNK,)),
        dma((3, NCHUNK)),
    ]
    grads = pl.pallas_call(
        kernel,
        out_shape=out_shape,
        in_specs=in_specs,
        out_specs=[any_spec] * 6,
        scratch_shapes=scratch,
        compiler_params=pltpu.CompilerParams(
            collective_id=0, has_side_effects=True, vmem_limit_bytes=60 * 1024 * 1024
        ),
        name="attention_backward",
    )(*args)
    return tuple(
        pl.pallas_call(
            emit,
            out_shape=out_shape,
            in_specs=[any_spec] * 6,
            out_specs=[any_spec] * 6,
            scratch_shapes=[pltpu.VMEM(out.shape, bf16) for out in out_shape] + [dma((6,)), dma((6,))],
            compiler_params=pltpu.CompilerParams(vmem_limit_bytes=60 * 1024 * 1024),
            name="emit",
        )(*grads)
    )


def solution(mesh):
    seq = P("dp", "ctx", None)
    slot = P("dp", "ctx", None, None)
    return jax.shard_map(
        body,
        mesh=mesh,
        in_specs=(seq,) * 5 + (P("dp", None),) + (slot,) * 5 + (P("dp", "ctx"),) * 2,
        out_specs=(seq, seq, seq, slot, slot, slot),
        check_vma=False,
    )
```

```python
import math

import jax
import jax.numpy as jnp
from jax import lax
from jax.experimental import pallas as pl
from jax.experimental.pallas import tpu as pltpu
from jax.sharding import PartitionSpec as P

H = 6
DH = 128
CH = 128
NZ = 8
NCTX = 16
NCHUNK = 32
NDOC = 4
SLOTS = 4
HC = H * DH
PAIRS = tuple(range(0, HC, 2 * DH))
SCALE = 1.0 / math.sqrt(DH)
SCALE2 = SCALE * math.log2(math.e)
NEG = -1e30
LAST_STEP = 4

HOPS_UP = {
    (0, 0, 0): (3, 3, 4, 4, 3, 2, 1, 0),
    (0, 0, 1): (0, 0, 0, 0, 0, 3, 4, 4),
    (0, 1, 0): (0, 0, 4, 4, 0, 0, 0, 4),
    (0, 1, 1): (1, 4, 1, 3, 4, 4, 3, 4),
    (1, 0, 0): (4, 4, 4, 3, 4, 3, 4, 4),
    (1, 0, 1): (3, 0, 3, 0, 0, 3, 3, 3),
    (1, 1, 0): (4, 3, 3, 4, 3, 4, 4, 3),
    (1, 1, 1): (0, 0, 0, 0, 0, 0, 0, 0),
}
HOPS_DOWN = {
    (0, 0, 0): (4, 4, 3, 0, 0, 0, 3, 0),
    (0, 0, 1): (0, 1, 2, 3, 4, 4, 3, 3),
    (0, 1, 0): (1, 3, 0, 0, 1, 0, 4, 2),
    (0, 1, 1): (4, 3, 4, 4, 3, 3, 4, 1),
    (1, 0, 0): (3, 3, 3, 4, 3, 4, 3, 3),
    (1, 0, 1): (0, 1, 2, 3, 4, 4, 4, 4),
    (1, 1, 0): (3, 4, 4, 3, 4, 3, 0, 4),
    (1, 1, 1): (0, 0, 0, 0, 0, 0, 0, 0),
}


def needed(j, c):
    return j <= c or 15 - c <= j <= 31 - c


def device_masks(c):
    x, z = divmod(c, NZ)
    across = (1 - x) * NZ + z
    hops = (HOPS_UP, HOPS_DOWN)

    def chunk(plane, late, zr):
        owner = plane * NZ + zr
        return 2 * NCTX - 1 - owner if late else owner

    def over_x(plane, late, way, step, to):
        zr = (z + step if way else z - step) % NZ
        near, far = hops[way][1 - plane, 1, late][zr], hops[1 - way][1 - plane, 1, late][zr]
        there = hops[way][plane, 0, late][zr]
        return there >= step and near < step and far < NZ - step and needed(chunk(plane, late, zr), to)

    def root_over_x(plane, late, to):
        on = hops[0][1 - plane, 1, late][z] + hops[1][1 - plane, 1, late][z]
        return on >= 1 or needed(chunk(plane, late, z), to)

    has = forwards = over = root = 0
    for late in (0, 1):
        root |= root_over_x(x, late, across) << late
        root |= root_over_x(1 - x, late, c) << (2 + late)
        for way in (0, 1):
            for foreign in (0, 1):
                n = 4 * foreign + 2 * late + way
                root |= (hops[way][x, foreign, late][z] >= 1) << (4 + n)
                for step in range(1, LAST_STEP + 1):
                    zr = (z + step if way else z - step) % NZ
                    reach = hops[way][x, foreign, late][zr]
                    has |= (reach >= step) << (8 * (step - 1) + n)
                    forwards |= (reach >= step + 1) << (8 * (step - 1) + n)
            for step in range(1, LAST_STEP + 1):
                bit = 4 * (step - 1) + 2 * late + way
                over |= over_x(x, late, way, step, across) << bit
                over |= over_x(1 - x, late, way, step, c) << (16 + bit)
    return tuple(m - (1 << 32) if m >= 1 << 31 else m for m in (has, forwards, over, root))


def nt(a, b):
    return lax.dot_general(a, b, (((1,), (1,)), ((), ())), preferred_element_type=jnp.float32)


def nn(a, b):
    return lax.dot_general(a, b, (((1,), (0,)), ((), ())), preferred_element_type=jnp.float32)


def heads(ref, col):
    return jnp.concatenate([ref[:, col : col + DH], ref[:, col + DH : col + 2 * DH]], axis=0)


def row_delta(grads, outs):
    prod = grads.astype(jnp.float32) * outs.astype(jnp.float32)
    high = prod.astype(jnp.bfloat16)
    low = (prod - high.astype(jnp.float32)).astype(jnp.bfloat16)
    ones = jnp.ones((16, DH), jnp.bfloat16)
    return (nt(ones, high) + nt(ones, low))[0:1]


def kernel(
    q_hbm, k_hbm, v_hbm, o_hbm, do_hbm, doc_ref,
    qs_hbm, ks_hbm, vs_hbm, os_hbm, dos_hbm, slen_ref, scount_ref,
    dq_out, dk_out, dv_out, dqs_out, dks_out, dvs_out,
    kv, q_v, o_v, do_v, qt_v, dot_v, scores, ds_v, m_v, l_v, lse_v, delta_v, lo_v, dqt, acc, held,
    snd, rcv, qs_v, ks_v, vs_v, os_v, dos_v,
    in_sem, ag_send, ag_recv, rs_send, rs_recv,
):
    f32, bf16 = jnp.float32, jnp.bfloat16
    c = lax.axis_index("ctx")
    x = c // NZ
    z = c - x * NZ
    late_own = 2 * NCTX - 1 - c
    z_up = lax.rem(z + 1, NZ)
    z_down = lax.rem(z + NZ - 1, NZ)
    across = (1 - x) * NZ + z
    beside = (x * NZ + z_up, x * NZ + z_down)

    masks = [jnp.int32(m) for m in device_masks(0)]
    for device in range(1, NCTX):
        here = c == device
        masks = [jnp.where(here, jnp.int32(m), old) for m, old in zip(device_masks(device), masks)]
    has_mask, forward_mask, over_mask, root_mask = masks

    def bit(mask, n):
        return ((mask >> n) & 1) == 1

    def has(step, n):
        return bit(has_mask, 8 * (step - 1) + n)

    def forwards(step, n):
        return bit(forward_mask, 8 * (step - 1) + n)

    def goes_across(step, n):
        return bit(over_mask, 4 * (step - 1) + n)

    def comes_across(step, n):
        return bit(over_mask, 16 + 4 * (step - 1) + n)

    def crosses(late):
        return bit(root_mask, late)

    def arrives(late):
        return bit(root_mask, 2 + late)

    def sets_out(foreign, late, way):
        return bit(root_mask, 4 + 4 * foreign + 2 * late + way)

    def choose(flag, one, zero):
        if isinstance(flag, int):
            return one if flag else zero
        return jnp.where(flag == 1, one, zero)

    def chunk_of(foreign, late, z_root):
        owner = (x + foreign * (1 - 2 * x)) * NZ + z_root
        return owner + late * (2 * NCTX - 1 - 2 * owner)

    def root_of(way, step):
        return (z + NZ + step * (2 * way - 1)) & (NZ - 1)

    def early_needs(j, who=c):
        return j <= who

    def late_needs(j, who=c):
        return (j >= 15 - who) & (j <= 2 * NCTX - 1 - who)

    def ag_copy(j, way, target):
        return pltpu.make_async_remote_copy(
            src_ref=kv.at[j], dst_ref=kv.at[j], send_sem=ag_send.at[j, way], recv_sem=ag_recv.at[j],
            device_id={"ctx": target}, device_id_type=pl.DeviceIdType.MESH,
        )

    def rs_copy(j, way, target):
        return pltpu.make_async_remote_copy(
            src_ref=snd.at[j], dst_ref=rcv.at[way, j], send_sem=rs_send.at[j], recv_sem=rs_recv.at[way, j],
            device_id={"ctx": target}, device_id_type=pl.DeviceIdType.MESH,
        )

    kv_loads = [
        pltpu.make_async_copy(src.at[0, pl.ds(half * CH, CH)], kv.at[j, which], in_sem.at[2 * which + half])
        for which, src in ((0, k_hbm), (1, v_hbm))
        for half, j in ((0, c), (1, late_own))
    ]
    long_loads = [
        pltpu.make_async_copy(src.at[0], dst, in_sem.at[4 + n])
        for n, (src, dst) in enumerate(((q_hbm, q_v), (do_hbm, do_v), (o_hbm, o_v)))
    ]
    short_loads = [
        pltpu.make_async_copy(src.at[0], dst, in_sem.at[7 + n])
        for n, (src, dst) in enumerate(
            ((qs_hbm, qs_v), (ks_hbm, ks_v), (vs_hbm, vs_v), (os_hbm, os_v), (dos_hbm, dos_v))
        )
    ]
    for copy in kv_loads + long_loads + short_loads:
        copy.start()

    barrier = pltpu.get_barrier_semaphore()
    for target in beside + (across,):
        pl.semaphore_signal(
            barrier, inc=1, device_id={"ctx": target}, device_id_type=pl.DeviceIdType.MESH
        )
    pl.semaphore_wait(barrier, 3)

    for copy in kv_loads:
        copy.wait()
    for late in (0, 1):
        j = chunk_of(0, late, z)

        @pl.when(crosses(late))
        def _():
            ag_copy(j, 2, across).start()

    for late in (0, 1):
        j = chunk_of(0, late, z)
        for way in (0, 1):

            @pl.when(sets_out(0, late, way))
            def _():
                ag_copy(j, way, beside[way]).start()

    for copy in long_loads:
        copy.wait()
    halves = [(pl.ds(half * CH, CH), own_chunk) for half, own_chunk in ((0, c), (1, late_own))]
    ends = []
    total = doc_ref[0, 0]
    for d in range(NDOC):
        ends.append(total)
        if d + 1 < NDOC:
            total = total + doc_ref[0, d + 1]
    lane = lax.rem(lax.broadcasted_iota(jnp.int32, (1, 2 * DH), 1), CH)
    sub = lax.broadcasted_iota(jnp.int32, (CH, 1), 0)
    for half, (rows, own_chunk) in enumerate(halves):
        pos = own_chunk * CH + lane
        first = jnp.zeros((1, 2 * DH), jnp.int32)
        for end in ends:
            first = jnp.maximum(first, jnp.where(pos >= end, end, 0))
        lo_v[half] = first
        for col in PAIRS:
            delta_v[half, :, col : col + 2 * DH] = row_delta(heads(do_v.at[rows], col), heads(o_v.at[rows], col))
        for col in range(0, HC, DH):
            qt_v[half, :, col : col + DH] = q_v[rows, col : col + DH].T
            dot_v[half, :, col : col + DH] = do_v[rows, col : col + DH].T
        m_v[half] = jnp.full((8, HC), NEG, f32)
        l_v[half] = jnp.zeros((8, HC), f32)
    dqt[0] = jnp.zeros((DH, HC), f32)

    def slot_of(half, j):
        return j if half == 0 else NCTX + j - (15 - c)

    def score_tiles(which, j):
        keys = kv[j, 0]
        key_pos = j * CH + sub
        for half in which:
            own_chunk = halves[half][1]
            visible = (key_pos >= lo_v[half]) & (key_pos <= own_chunk * CH + lane)
            bias = jnp.where(visible, 0.0, NEG)
            slot = slot_of(half, j)
            for col in PAIRS:
                cols = slice(col, col + 2 * DH)
                s = nn(keys, qt_v[half, :, cols]) * SCALE2 + bias
                scores[slot, :, cols] = s
                s = s.reshape(CH // 8, 8, 2 * DH)
                m_old = m_v[half, :, cols]
                m_new = jnp.maximum(m_old, jnp.max(s, axis=0))
                m_v[half, :, cols] = m_new
                l_v[half, :, cols] = l_v[half, :, cols] * jnp.exp2(m_old - m_new) + jnp.sum(
                    jnp.exp2(s - m_new[None]), axis=0
                )

    def for_needed(j, has, tiles):
        early, late = early_needs(j), late_needs(j)
        for which, wanted in (((0, 1), early & late), ((0,), early & ~late), ((1,), late & ~early)):

            @pl.when(has & wanted)
            def _():
                tiles(which, j)

    def score_item(j, has):
        for_needed(j, has, score_tiles)

    def short_slot(slot):
        length = jnp.where(slot < scount_ref[0, 0], slen_ref[0, slot], 0)
        keys = ks_v[slot]
        values = vs_v[slot]
        visible = (sub <= lane) & (lane < length)
        dk = jnp.zeros((CH, DH), f32)
        dv = jnp.zeros((CH, DH), f32)
        for col in PAIRS:
            queries = heads(qs_v.at[slot], col)
            grads = heads(dos_v.at[slot], col)
            delta = row_delta(grads, heads(os_v.at[slot], col))
            s = jnp.where(visible, nt(keys, queries) * SCALE2, NEG)
            e = jnp.exp2(s - jnp.max(s, axis=0, keepdims=True))
            inverse = jnp.where(lane < length, 1.0 / jnp.sum(e, axis=0, keepdims=True), 0.0)
            p = e * inverse
            ds = (p * (nt(values, grads) - delta)).astype(bf16)
            dv = dv + nn(p.astype(bf16), grads)
            dk = dk + nn(ds, queries)
            dq = lax.dot_general(keys, ds, (((0,), (0,)), ((), ())), preferred_element_type=f32)
            for n in (0, 1):
                dqs_out[0, slot, :, col + n * DH : col + (n + 1) * DH] = (
                    dq[:, n * DH : (n + 1) * DH].T * SCALE
                ).astype(bf16)
        dks_out[0, slot] = (dk * SCALE).astype(bf16)
        dvs_out[0, slot] = dv.astype(bf16)

    score_item(c, c >= 0)
    score_item(late_own, c >= 0)

    for late in (0, 1):
        j = chunk_of(1, late, z)

        @pl.when(arrives(late))
        def _():
            ag_copy(j, 2, across).wait_recv()
            for way in (0, 1):

                @pl.when(sets_out(1, late, way))
                def _():
                    ag_copy(j, way, beside[way]).start()

    def foreign_score(late, carry):
        score_item(chunk_of(1, late, z), arrives(late))
        return carry

    lax.fori_loop(0, 2, foreign_score, 0)

    for copy in short_loads:
        copy.wait()

    def score_across(step):
        def item(n, carry):
            j = chunk_of(1, n // 2, root_of(lax.rem(n, 2), step))

            @pl.when(comes_across(step, n))
            def _():
                ag_copy(j, 2, across).wait_recv()
                score_item(j, c >= 0)

            return carry

        @pl.when(step >= 1)
        def _():
            lax.fori_loop(0, 4, item, 0)

    def gather_step(step, carry):
        for n in range(8):
            foreign, late, way = n // 4, n // 2 % 2, n % 2
            j = chunk_of(foreign, late, root_of(way, step))

            @pl.when(has(step, n))
            def _():
                ag_copy(j, way, beside[way]).wait_recv()

            @pl.when(forwards(step, n))
            def _():
                ag_copy(j, way, beside[way]).start()

            if foreign == 0:

                @pl.when(goes_across(step, n))
                def _():
                    ag_copy(j, 2, across).start()

        short_slot(step - 1)

        def item(n, carry):
            foreign, late, way = n // 4, (n // 2) & 1, n & 1
            score_item(chunk_of(foreign, late, root_of(way, step)), has(step, n))
            return carry

        lax.fori_loop(0, 8, item, carry)
        score_across(step - 1)
        return carry

    lax.fori_loop(1, LAST_STEP + 1, gather_step, 0)
    score_across(LAST_STEP)

    for half in (0, 1):
        m = jnp.max(m_v[half], axis=0, keepdims=True)
        lse_v[half] = m + jnp.log2(jnp.sum(l_v[half] * jnp.exp2(m_v[half] - m), axis=0, keepdims=True))

    def grad_tiles(which, j):
        values = kv[j, 1]
        p_parts, ds_parts, q_parts, do_parts = [], [], [], []
        for half in which:
            rows, own_chunk = halves[half]
            slot = slot_of(half, j)
            for col in PAIRS:
                cols = slice(col, col + 2 * DH)
                grads = heads(do_v.at[rows], col)
                p = jnp.exp2(scores[slot, :, cols] - lse_v[half, :, cols])
                ds = (p * (nn(values, dot_v[half, :, cols]) - delta_v[half, :, cols])).astype(bf16)
                ds_v[slot, :, cols] = ds
                p_parts.append(p.astype(bf16))
                ds_parts.append(ds)
                q_parts.append(heads(q_v.at[rows], col))
                do_parts.append(grads)
        acc[0] = nn(jnp.concatenate(ds_parts, axis=1), jnp.concatenate(q_parts, axis=0))
        acc[1] = nn(jnp.concatenate(p_parts, axis=1), jnp.concatenate(do_parts, axis=0))

    def grad_item(j):
        @pl.when(~(early_needs(j) | late_needs(j)))
        def _():
            acc[...] = jnp.zeros((2, CH, DH), f32)

        for_needed(j, c >= 0, grad_tiles)

    def grads_across(step):
        def item(n, carry):
            j = chunk_of(1, n // 2, root_of(lax.rem(n, 2), step))

            @pl.when(comes_across(step, n))
            def _():
                grad_item(j)
                snd[j] = acc[...].astype(bf16)
                rs_copy(j, 2, across).start()

            return carry

        @pl.when(step >= 1)
        def _():
            lax.fori_loop(0, 4, item, 0)

    def add_term(way, j, target):
        rs_copy(j, way, target).wait_recv()
        acc[...] += rcv[way, j].astype(f32)

    def grads_of_roots(n, carry):
        foreign, late = n // 2, n & 1

        @pl.when((foreign == 0) | arrives(late))
        def _():
            grad_item(chunk_of(foreign, late, z))
            held[n] = acc[...]

        return carry

    def scatter_step(back, carry):
        step = LAST_STEP - back

        @pl.when(step == 1)
        def _():
            lax.fori_loop(0, 4, grads_of_roots, 0)

        grads_across(step - 1)

        def item(i, carry):
            n = (i + 4) & 7
            foreign, late, way = n // 4, (n // 2) & 1, n & 1
            j = chunk_of(foreign, late, root_of(way, step))

            @pl.when(has(step, n))
            def _():
                grad_item(j)

                @pl.when(forwards(step, n))
                def _():
                    add_term(way, j, beside[0])

                @pl.when((foreign == 0) & goes_across(step, n & 3))
                def _():
                    add_term(2, j, across)

                snd[j] = acc[...].astype(bf16)
                rs_copy(j, way, choose(way, beside[0], beside[1])).start()

            return carry

        return lax.fori_loop(0, 8, item, carry)

    grads_across(LAST_STEP)
    lax.fori_loop(0, LAST_STEP, scatter_step, 0)

    def collect(foreign, late, j):
        for way in (0, 1):

            @pl.when(sets_out(foreign, late, way))
            def _():
                add_term(way, j, beside[way])

    def foreign_root(late, carry):
        j = chunk_of(1, late, z)

        @pl.when(arrives(late))
        def _():
            acc[...] = held[2 + late]
            collect(1, late, j)
            snd[j] = acc[...].astype(bf16)
            rs_copy(j, 2, across).start()

        return carry

    lax.fori_loop(0, 2, foreign_root, 0)

    def tn(a, b):
        return lax.dot_general(a, b, (((0,), (0,)), ((), ())), preferred_element_type=f32)

    def dq_early(first, count):
        keys = kv[pl.ds(first, count), 0].reshape(count * CH, DH)
        for col in PAIRS:
            cols = slice(col, col + 2 * DH)
            dqt[0, :, cols] += tn(keys, ds_v[pl.ds(first, count), :, cols].reshape(count * CH, 2 * DH))

    def dq_early_two(n, carry):
        dq_early(2 * n, 2)
        return carry

    lax.fori_loop(0, (c + 1) // 2, dq_early_two, 0)

    @pl.when(lax.rem(c, 2) == 0)
    def _():
        dq_early(c, 1)

    keys = kv[pl.ds(15 - c, 17), 0].reshape(17 * CH, DH)
    for col in PAIRS:
        cols = slice(col, col + 2 * DH)
        dqt[1, :, cols] = tn(keys, ds_v[NCTX : NCTX + 17, :, cols].reshape(17 * CH, 2 * DH))
    for half, (rows, own_chunk) in enumerate(halves):
        for col in range(0, HC, DH):
            dq_out[0, rows, col : col + DH] = (dqt[half, :, col : col + DH].T * SCALE).astype(bf16)
    for late in (0, 1):
        j = chunk_of(0, late, z)

        @pl.when(crosses(late))
        def _():
            ag_copy(j, 2, across).wait_send()

        for foreign in (0, 1):
            j = chunk_of(foreign, late, z)
            for way in (0, 1):

                @pl.when(sets_out(foreign, late, way))
                def _():
                    ag_copy(j, way, beside[way]).wait_send()

        @pl.when(arrives(late))
        def _():
            rs_copy(chunk_of(1, late, z), 2, across).wait_send()

    def sent_step(step, carry):
        for n in range(8):
            foreign, late, way = n // 4, n // 2 % 2, n % 2
            j = chunk_of(foreign, late, root_of(way, step))

            @pl.when(has(step, n))
            def _():
                rs_copy(j, way, beside[0]).wait_send()

            @pl.when(forwards(step, n))
            def _():
                ag_copy(j, way, beside[0]).wait_send()

            if foreign == 0:

                @pl.when(goes_across(step, n))
                def _():
                    ag_copy(j, 2, across).wait_send()

            else:

                @pl.when(comes_across(step, n & 3))
                def _():
                    rs_copy(j, 2, across).wait_send()

        return carry

    lax.fori_loop(1, LAST_STEP + 1, sent_step, 0)

    def own_total(late, carry):
        acc[...] = held[late]
        j = chunk_of(0, late, z)
        collect(0, late, j)

        @pl.when(crosses(late))
        def _():
            add_term(2, j, across)

        rows = pl.ds(pl.multiple_of(late * CH, CH), CH)
        dk_out[0, rows] = (acc[0] * SCALE).astype(bf16)
        dv_out[0, rows] = acc[1].astype(bf16)
        return carry

    lax.fori_loop(0, 2, own_total, 0)

def emit(*refs):
    ins, outs, sem = refs[:6], refs[6:12], refs[12]
    copies = [pltpu.make_async_copy(ins[n], outs[n], sem.at[n]) for n in range(6)]
    for copy in copies:
        copy.start()
    for copy in copies:
        copy.wait()


def body(*args):
    bf16, f32 = jnp.bfloat16, jnp.float32
    tok = args[0].shape[1]
    any_spec = pl.BlockSpec(memory_space=pltpu.HBM)
    smem_spec = pl.BlockSpec(memory_space=pltpu.SMEM)
    in_specs = [any_spec] * 5 + [smem_spec] + [any_spec] * 5 + [smem_spec] * 2
    out_shape = [jax.ShapeDtypeStruct(args[n].shape, bf16) for n in (0, 1, 2, 6, 7, 8)]
    dma = pltpu.SemaphoreType.DMA
    scratch = [
        pltpu.VMEM((NCHUNK, 2, CH, DH), bf16),
        pltpu.VMEM((tok, HC), bf16),
        pltpu.VMEM((tok, HC), bf16),
        pltpu.VMEM((tok, HC), bf16),
        pltpu.VMEM((2, DH, HC), bf16),
        pltpu.VMEM((2, DH, HC), bf16),
        pltpu.VMEM((33, CH, HC), f32),
        pltpu.VMEM((33, CH, HC), bf16),
        pltpu.VMEM((2, 8, HC), f32),
        pltpu.VMEM((2, 8, HC), f32),
        pltpu.VMEM((2, 1, HC), f32),
        pltpu.VMEM((2, 1, HC), f32),
        pltpu.VMEM((2, 1, 2 * DH), jnp.int32),
        pltpu.VMEM((2, DH, HC), f32),
        pltpu.VMEM((2, CH, DH), f32),
        pltpu.VMEM((4, 2, CH, DH), f32),
        pltpu.VMEM((NCHUNK, 2, CH, DH), bf16),
        pltpu.VMEM((3, NCHUNK, 2, CH, DH), bf16),
        pltpu.VMEM((SLOTS, CH, HC), bf16),
        pltpu.VMEM((SLOTS, CH, DH), bf16),
        pltpu.VMEM((SLOTS, CH, DH), bf16),
        pltpu.VMEM((SLOTS, CH, HC), bf16),
        pltpu.VMEM((SLOTS, CH, HC), bf16),
        dma((12,)),
        dma((NCHUNK, 3)),
        dma((NCHUNK,)),
        dma((NCHUNK,)),
        dma((3, NCHUNK)),
    ]
    grads = pl.pallas_call(
        kernel,
        out_shape=[pltpu.VMEM(out.shape, out.dtype) for out in out_shape],
        in_specs=in_specs,
        out_specs=[pl.BlockSpec(memory_space=pltpu.VMEM)] * 6,
        scratch_shapes=scratch,
        compiler_params=pltpu.CompilerParams(
            collective_id=0, has_side_effects=True, vmem_limit_bytes=56 * 1024 * 1024
        ),
        name="attention_backward",
    )(*args)
    return tuple(
        pl.pallas_call(
            emit,
            out_shape=out_shape,
            in_specs=[pl.BlockSpec(memory_space=pltpu.VMEM)] * 6,
            out_specs=[any_spec] * 6,
            scratch_shapes=[dma((6,))],
            name="emit",
        )(*grads)
    )


def solution(mesh):
    seq = P("dp", "ctx", None)
    slot = P("dp", "ctx", None, None)
    return jax.shard_map(
        body,
        mesh=mesh,
        in_specs=(seq,) * 5 + (P("dp", None),) + (slot,) * 5 + (P("dp", "ctx"),) * 2,
        out_specs=(seq, seq, seq, slot, slot, slot),
        check_vma=False,
    )
```

```python
import math

import jax
import jax.numpy as jnp
from jax import lax
from jax.experimental import pallas as pl
from jax.experimental.pallas import tpu as pltpu
from jax.sharding import PartitionSpec as P

H = 6
DH = 128
CH = 128
NZ = 8
NCTX = 16
NCHUNK = 32
NDOC = 4
SLOTS = 4
HC = H * DH
PAIRS = tuple(range(0, HC, 2 * DH))
SCALE = 1.0 / math.sqrt(DH)
SCALE2 = SCALE * math.log2(math.e)
NEG = -1e30
LAST_STEP = 4

HOPS_UP = {
    (0, 0, 0): (4, 4, 3, 4, 3, 2, 1, 0),
    (0, 0, 1): (0, 0, 0, 0, 0, 3, 4, 4),
    (0, 1, 0): (0, 0, 0, 4, 0, 0, 1, 4),
    (0, 1, 1): (4, 3, 4, 4, 3, 4, 0, 4),
    (1, 0, 0): (4, 3, 4, 4, 3, 4, 4, 4),
    (1, 0, 1): (0, 0, 0, 0, 0, 4, 4, 4),
    (1, 1, 0): (4, 2, 3, 4, 4, 3, 3, 4),
    (1, 1, 1): (0, 0, 0, 0, 0, 0, 0, 0),
}
HOPS_DOWN = {
    (0, 0, 0): (3, 3, 4, 3, 0, 0, 0, 0),
    (0, 0, 1): (0, 1, 2, 3, 4, 4, 3, 3),
    (0, 1, 0): (0, 0, 4, 0, 0, 0, 4, 0),
    (0, 1, 1): (3, 4, 3, 2, 4, 3, 4, 3),
    (1, 0, 0): (3, 4, 3, 3, 4, 3, 3, 3),
    (1, 0, 1): (0, 1, 2, 3, 4, 3, 3, 3),
    (1, 1, 0): (3, 4, 4, 2, 3, 4, 4, 3),
    (1, 1, 1): (0, 0, 0, 0, 0, 0, 0, 0),
}


def needed(j, c):
    return j <= c or 15 - c <= j <= 31 - c


def device_masks(c):
    x, z = divmod(c, NZ)
    across = (1 - x) * NZ + z
    hops = (HOPS_UP, HOPS_DOWN)

    def chunk(plane, late, zr):
        owner = plane * NZ + zr
        return 2 * NCTX - 1 - owner if late else owner

    def over_x(plane, late, way, step, to):
        zr = (z + step if way else z - step) % NZ
        near, far = hops[way][1 - plane, 1, late][zr], hops[1 - way][1 - plane, 1, late][zr]
        there = hops[way][plane, 0, late][zr]
        return there >= step and near < step and far < NZ - step and needed(chunk(plane, late, zr), to)

    def root_over_x(plane, late, to):
        on = hops[0][1 - plane, 1, late][z] + hops[1][1 - plane, 1, late][z]
        return on >= 1 or needed(chunk(plane, late, z), to)

    has = forwards = over = root = 0
    for late in (0, 1):
        root |= root_over_x(x, late, across) << late
        root |= root_over_x(1 - x, late, c) << (2 + late)
        for way in (0, 1):
            for foreign in (0, 1):
                n = 4 * foreign + 2 * late + way
                root |= (hops[way][x, foreign, late][z] >= 1) << (4 + n)
                for step in range(1, LAST_STEP + 1):
                    zr = (z + step if way else z - step) % NZ
                    reach = hops[way][x, foreign, late][zr]
                    has |= (reach >= step) << (8 * (step - 1) + n)
                    forwards |= (reach >= step + 1) << (8 * (step - 1) + n)
            for step in range(1, LAST_STEP + 1):
                bit = 4 * (step - 1) + 2 * late + way
                over |= over_x(x, late, way, step, across) << bit
                over |= over_x(1 - x, late, way, step, c) << (16 + bit)
    return tuple(m - (1 << 32) if m >= 1 << 31 else m for m in (has, forwards, over, root))


def nt(a, b):
    return lax.dot_general(a, b, (((1,), (1,)), ((), ())), preferred_element_type=jnp.float32)


def nn(a, b):
    return lax.dot_general(a, b, (((1,), (0,)), ((), ())), preferred_element_type=jnp.float32)


def heads(ref, col):
    return jnp.concatenate([ref[:, col : col + DH], ref[:, col + DH : col + 2 * DH]], axis=0)


def row_delta(grads, outs):
    prod = grads.astype(jnp.float32) * outs.astype(jnp.float32)
    high = prod.astype(jnp.bfloat16)
    low = (prod - high.astype(jnp.float32)).astype(jnp.bfloat16)
    ones = jnp.ones((16, DH), jnp.bfloat16)
    return (nt(ones, high) + nt(ones, low))[0:1]


def kernel(
    q_hbm, k_hbm, v_hbm, o_hbm, do_hbm, doc_ref,
    qs_hbm, ks_hbm, vs_hbm, os_hbm, dos_hbm, slen_ref, scount_ref,
    dq_hbm, dk_hbm, dv_hbm, dqs_hbm, dks_hbm, dvs_hbm,
    kv, q_v, o_v, do_v, qt_v, dot_v, scores, ds_v, m_v, l_v, lse_v, delta_v, lo_v, dqt, acc, held,
    snd, rcv, qs_v, ks_v, vs_v, os_v, dos_v, dq_v, dkv_v, dqs_v, dks_v, dvs_v,
    in_sem, out_sem, ag_send, ag_recv, rs_send, rs_recv,
):
    f32, bf16 = jnp.float32, jnp.bfloat16
    c = lax.axis_index("ctx")
    x = c // NZ
    z = c - x * NZ
    late_own = 2 * NCTX - 1 - c
    z_up = lax.rem(z + 1, NZ)
    z_down = lax.rem(z + NZ - 1, NZ)
    across = (1 - x) * NZ + z
    beside = (x * NZ + z_up, x * NZ + z_down)

    masks = [jnp.int32(m) for m in device_masks(0)]
    for device in range(1, NCTX):
        here = c == device
        masks = [jnp.where(here, jnp.int32(m), old) for m, old in zip(device_masks(device), masks)]
    has_mask, forward_mask, over_mask, root_mask = masks

    def bit(mask, n):
        return ((mask >> n) & 1) == 1

    def has(step, n):
        return bit(has_mask, 8 * (step - 1) + n)

    def forwards(step, n):
        return bit(forward_mask, 8 * (step - 1) + n)

    def goes_across(step, n):
        return bit(over_mask, 4 * (step - 1) + n)

    def comes_across(step, n):
        return bit(over_mask, 16 + 4 * (step - 1) + n)

    def crosses(late):
        return bit(root_mask, late)

    def arrives(late):
        return bit(root_mask, 2 + late)

    def sets_out(foreign, late, way):
        return bit(root_mask, 4 + 4 * foreign + 2 * late + way)

    def choose(flag, one, zero):
        if isinstance(flag, int):
            return one if flag else zero
        return jnp.where(flag == 1, one, zero)

    def chunk_of(foreign, late, z_root):
        owner = (x + foreign * (1 - 2 * x)) * NZ + z_root
        return owner + late * (2 * NCTX - 1 - 2 * owner)

    def root_of(way, step):
        return (z + NZ + step * (2 * way - 1)) & (NZ - 1)

    def early_needs(j, who=c):
        return j <= who

    def late_needs(j, who=c):
        return (j >= 15 - who) & (j <= 2 * NCTX - 1 - who)

    def ag_copy(j, way, target):
        return pltpu.make_async_remote_copy(
            src_ref=kv.at[j], dst_ref=kv.at[j], send_sem=ag_send.at[j, way], recv_sem=ag_recv.at[j],
            device_id={"ctx": target}, device_id_type=pl.DeviceIdType.MESH,
        )

    def rs_copy(j, way, target):
        return pltpu.make_async_remote_copy(
            src_ref=snd.at[j], dst_ref=rcv.at[way, j], send_sem=rs_send.at[j], recv_sem=rs_recv.at[way, j],
            device_id={"ctx": target}, device_id_type=pl.DeviceIdType.MESH,
        )

    kv_loads = [
        pltpu.make_async_copy(src.at[0, pl.ds(half * CH, CH)], kv.at[j, which], in_sem.at[2 * which + half])
        for which, src in ((0, k_hbm), (1, v_hbm))
        for half, j in ((0, c), (1, late_own))
    ]
    long_loads = [
        pltpu.make_async_copy(src.at[0], dst, in_sem.at[4 + n])
        for n, (src, dst) in enumerate(((q_hbm, q_v), (do_hbm, do_v), (o_hbm, o_v)))
    ]
    short_loads = [
        pltpu.make_async_copy(src.at[0], dst, in_sem.at[7 + n])
        for n, (src, dst) in enumerate(
            ((qs_hbm, qs_v), (ks_hbm, ks_v), (vs_hbm, vs_v), (os_hbm, os_v), (dos_hbm, dos_v))
        )
    ]
    for copy in kv_loads + long_loads + short_loads:
        copy.start()

    barrier = pltpu.get_barrier_semaphore()
    for target in beside + (across,):
        pl.semaphore_signal(
            barrier, inc=1, device_id={"ctx": target}, device_id_type=pl.DeviceIdType.MESH
        )
    pl.semaphore_wait(barrier, 3)

    for copy in kv_loads:
        copy.wait()
    for late in (0, 1):
        j = chunk_of(0, late, z)

        @pl.when(crosses(late))
        def _():
            ag_copy(j, 2, across).start()

    for late in (0, 1):
        j = chunk_of(0, late, z)
        for way in (0, 1):

            @pl.when(sets_out(0, late, way))
            def _():
                ag_copy(j, way, beside[way]).start()

    for copy in long_loads:
        copy.wait()
    halves = [(pl.ds(half * CH, CH), own_chunk) for half, own_chunk in ((0, c), (1, late_own))]
    ends = []
    total = doc_ref[0, 0]
    for d in range(NDOC):
        ends.append(total)
        if d + 1 < NDOC:
            total = total + doc_ref[0, d + 1]
    lane = lax.rem(lax.broadcasted_iota(jnp.int32, (1, 2 * DH), 1), CH)
    sub = lax.broadcasted_iota(jnp.int32, (CH, 1), 0)
    for half, (rows, own_chunk) in enumerate(halves):
        pos = own_chunk * CH + lane
        first = jnp.zeros((1, 2 * DH), jnp.int32)
        for end in ends:
            first = jnp.maximum(first, jnp.where(pos >= end, end, 0))
        lo_v[half] = first
        for col in PAIRS:
            delta_v[half, :, col : col + 2 * DH] = row_delta(heads(do_v.at[rows], col), heads(o_v.at[rows], col))
        for col in range(0, HC, DH):
            qt_v[half, :, col : col + DH] = q_v[rows, col : col + DH].T
            dot_v[half, :, col : col + DH] = do_v[rows, col : col + DH].T
        m_v[half] = jnp.full((8, HC), NEG, f32)
        l_v[half] = jnp.zeros((8, HC), f32)
    dqt[0] = jnp.zeros((DH, HC), f32)

    def slot_of(half, j):
        return j if half == 0 else NCTX + j - (15 - c)

    def score_tiles(which, j):
        keys = kv[j, 0]
        key_pos = j * CH + sub
        for half in which:
            own_chunk = halves[half][1]
            visible = (key_pos >= lo_v[half]) & (key_pos <= own_chunk * CH + lane)
            bias = jnp.where(visible, 0.0, NEG)
            slot = slot_of(half, j)
            for col in PAIRS:
                cols = slice(col, col + 2 * DH)
                s = nn(keys, qt_v[half, :, cols]) * SCALE2 + bias
                scores[slot, :, cols] = s
                s = s.reshape(CH // 8, 8, 2 * DH)
                m_old = m_v[half, :, cols]
                m_new = jnp.maximum(m_old, jnp.max(s, axis=0))
                m_v[half, :, cols] = m_new
                l_v[half, :, cols] = l_v[half, :, cols] * jnp.exp2(m_old - m_new) + jnp.sum(
                    jnp.exp2(s - m_new[None]), axis=0
                )

    def for_needed(j, has, tiles):
        early, late = early_needs(j), late_needs(j)
        for which, wanted in (((0, 1), early & late), ((0,), early & ~late), ((1,), late & ~early)):

            @pl.when(has & wanted)
            def _():
                tiles(which, j)

    def score_item(j, has):
        for_needed(j, has, score_tiles)

    def short_slot(slot):
        length = jnp.where(slot < scount_ref[0, 0], slen_ref[0, slot], 0)
        keys = ks_v[slot]
        values = vs_v[slot]
        visible = (sub <= lane) & (lane < length)
        dk = jnp.zeros((CH, DH), f32)
        dv = jnp.zeros((CH, DH), f32)
        for col in PAIRS:
            queries = heads(qs_v.at[slot], col)
            grads = heads(dos_v.at[slot], col)
            delta = row_delta(grads, heads(os_v.at[slot], col))
            s = jnp.where(visible, nt(keys, queries) * SCALE2, NEG)
            e = jnp.exp2(s - jnp.max(s, axis=0, keepdims=True))
            inverse = jnp.where(lane < length, 1.0 / jnp.sum(e, axis=0, keepdims=True), 0.0)
            p = e * inverse
            ds = (p * (nt(values, grads) - delta)).astype(bf16)
            dv = dv + nn(p.astype(bf16), grads)
            dk = dk + nn(ds, queries)
            dq = lax.dot_general(keys, ds, (((0,), (0,)), ((), ())), preferred_element_type=f32)
            for n in (0, 1):
                dqs_v[slot, :, col + n * DH : col + (n + 1) * DH] = (
                    dq[:, n * DH : (n + 1) * DH].T * SCALE
                ).astype(bf16)
        dks_v[slot] = (dk * SCALE).astype(bf16)
        dvs_v[slot] = dv.astype(bf16)

    score_item(c, c >= 0)
    score_item(late_own, c >= 0)

    for late in (0, 1):
        j = chunk_of(1, late, z)

        @pl.when(arrives(late))
        def _():
            ag_copy(j, 2, across).wait_recv()
            for way in (0, 1):

                @pl.when(sets_out(1, late, way))
                def _():
                    ag_copy(j, way, beside[way]).start()

    def foreign_score(late, carry):
        score_item(chunk_of(1, late, z), arrives(late))
        return carry

    lax.fori_loop(0, 2, foreign_score, 0)

    for copy in short_loads:
        copy.wait()

    def score_across(step):
        def item(n, carry):
            j = chunk_of(1, n // 2, root_of(lax.rem(n, 2), step))

            @pl.when(comes_across(step, n))
            def _():
                ag_copy(j, 2, across).wait_recv()
                score_item(j, c >= 0)

            return carry

        @pl.when(step >= 1)
        def _():
            lax.fori_loop(0, 4, item, 0)

    def gather_step(step, carry):
        def pair(q, carry):
            foreign, late = q // 2, q & 1
            for way in (0, 1):
                j = chunk_of(foreign, late, root_of(way, step))

                @pl.when(has(step, 2 * q + way))
                def _():
                    ag_copy(j, way, beside[way]).wait_recv()

                @pl.when(forwards(step, 2 * q + way))
                def _():
                    ag_copy(j, way, beside[way]).start()

                @pl.when((foreign == 0) & goes_across(step, (2 * q + way) & 3))
                def _():
                    ag_copy(j, 2, across).start()

            @pl.when(q == 0)
            def _():
                short_slot(step - 1)

            def item(way, carry):
                score_item(chunk_of(foreign, late, root_of(way, step)), has(step, 2 * q + way))
                return carry

            return lax.fori_loop(0, 2, item, carry)

        lax.fori_loop(0, 4, pair, carry)
        score_across(step - 1)
        return carry

    lax.fori_loop(1, LAST_STEP + 1, gather_step, 0)
    score_across(LAST_STEP)

    short_stores = [
        pltpu.make_async_copy(src, dst.at[0], out_sem.at[n])
        for n, (src, dst) in enumerate(((dqs_v, dqs_hbm), (dks_v, dks_hbm), (dvs_v, dvs_hbm)))
    ]
    for copy in short_stores:
        copy.start()

    for half in (0, 1):
        m = jnp.max(m_v[half], axis=0, keepdims=True)
        lse_v[half] = m + jnp.log2(jnp.sum(l_v[half] * jnp.exp2(m_v[half] - m), axis=0, keepdims=True))

    def grad_tiles(which, j):
        values = kv[j, 1]
        p_parts, ds_parts, q_parts, do_parts = [], [], [], []
        for half in which:
            rows, own_chunk = halves[half]
            slot = slot_of(half, j)
            for col in PAIRS:
                cols = slice(col, col + 2 * DH)
                grads = heads(do_v.at[rows], col)
                p = jnp.exp2(scores[slot, :, cols] - lse_v[half, :, cols])
                ds = (p * (nn(values, dot_v[half, :, cols]) - delta_v[half, :, cols])).astype(bf16)
                ds_v[slot, :, cols] = ds
                p_parts.append(p.astype(bf16))
                ds_parts.append(ds)
                q_parts.append(heads(q_v.at[rows], col))
                do_parts.append(grads)
        acc[0] = nn(jnp.concatenate(ds_parts, axis=1), jnp.concatenate(q_parts, axis=0))
        acc[1] = nn(jnp.concatenate(p_parts, axis=1), jnp.concatenate(do_parts, axis=0))

    def grad_item(j):
        @pl.when(~(early_needs(j) | late_needs(j)))
        def _():
            acc[...] = jnp.zeros((2, CH, DH), f32)

        for_needed(j, c >= 0, grad_tiles)

    def grads_across(step):
        def item(n, carry):
            j = chunk_of(1, n // 2, root_of(lax.rem(n, 2), step))

            @pl.when(comes_across(step, n))
            def _():
                grad_item(j)
                snd[j] = acc[...].astype(bf16)
                rs_copy(j, 2, across).start()

            return carry

        @pl.when(step >= 1)
        def _():
            lax.fori_loop(0, 4, item, 0)

    def add_term(way, j, target):
        rs_copy(j, way, target).wait_recv()
        acc[...] += rcv[way, j].astype(f32)

    def grads_of_roots(n, carry):
        foreign, late = n // 2, n & 1

        @pl.when((foreign == 0) | arrives(late))
        def _():
            grad_item(chunk_of(foreign, late, z))
            held[n] = acc[...]

        return carry

    def scatter_step(back, carry):
        step = LAST_STEP - back

        @pl.when(step == 1)
        def _():
            lax.fori_loop(0, 4, grads_of_roots, 0)

        grads_across(step - 1)

        def item(i, carry):
            n = (i + 4) & 7
            foreign, late, way = n // 4, (n // 2) & 1, n & 1
            j = chunk_of(foreign, late, root_of(way, step))

            @pl.when(has(step, n))
            def _():
                grad_item(j)

                @pl.when(forwards(step, n))
                def _():
                    add_term(way, j, beside[0])

                @pl.when((foreign == 0) & goes_across(step, n & 3))
                def _():
                    add_term(2, j, across)

                snd[j] = acc[...].astype(bf16)
                rs_copy(j, way, choose(way, beside[0], beside[1])).start()

            return carry

        return lax.fori_loop(0, 8, item, carry)

    grads_across(LAST_STEP)
    lax.fori_loop(0, LAST_STEP, scatter_step, 0)

    def collect(foreign, late, j):
        for way in (0, 1):

            @pl.when(sets_out(foreign, late, way))
            def _():
                add_term(way, j, beside[way])

    def foreign_root(late, carry):
        j = chunk_of(1, late, z)

        @pl.when(arrives(late))
        def _():
            acc[...] = held[2 + late]
            collect(1, late, j)
            snd[j] = acc[...].astype(bf16)
            rs_copy(j, 2, across).start()

        return carry

    lax.fori_loop(0, 2, foreign_root, 0)

    def tn(a, b):
        return lax.dot_general(a, b, (((0,), (0,)), ((), ())), preferred_element_type=f32)

    def dq_early(first, count):
        keys = kv[pl.ds(first, count), 0].reshape(count * CH, DH)
        for col in PAIRS:
            cols = slice(col, col + 2 * DH)
            dqt[0, :, cols] += tn(keys, ds_v[pl.ds(first, count), :, cols].reshape(count * CH, 2 * DH))

    def dq_early_two(n, carry):
        dq_early(2 * n, 2)
        return carry

    lax.fori_loop(0, (c + 1) // 2, dq_early_two, 0)

    @pl.when(lax.rem(c, 2) == 0)
    def _():
        dq_early(c, 1)

    keys = kv[pl.ds(15 - c, 17), 0].reshape(17 * CH, DH)
    for col in PAIRS:
        cols = slice(col, col + 2 * DH)
        dqt[1, :, cols] = tn(keys, ds_v[NCTX : NCTX + 17, :, cols].reshape(17 * CH, 2 * DH))
    for half, (rows, own_chunk) in enumerate(halves):
        for col in range(0, HC, DH):
            dq_v[rows, col : col + DH] = (dqt[half, :, col : col + DH].T * SCALE).astype(bf16)
    dq_store = pltpu.make_async_copy(dq_v, dq_hbm.at[0], out_sem.at[3])
    dq_store.start()

    for late in (0, 1):
        j = chunk_of(0, late, z)

        @pl.when(crosses(late))
        def _():
            ag_copy(j, 2, across).wait_send()

        for foreign in (0, 1):
            j = chunk_of(foreign, late, z)
            for way in (0, 1):

                @pl.when(sets_out(foreign, late, way))
                def _():
                    ag_copy(j, way, beside[way]).wait_send()

        @pl.when(arrives(late))
        def _():
            rs_copy(chunk_of(1, late, z), 2, across).wait_send()

    def sent_step(step, carry):
        for n in range(8):
            foreign, late, way = n // 4, n // 2 % 2, n % 2
            j = chunk_of(foreign, late, root_of(way, step))

            @pl.when(has(step, n))
            def _():
                rs_copy(j, way, beside[0]).wait_send()

            @pl.when(forwards(step, n))
            def _():
                ag_copy(j, way, beside[0]).wait_send()

            if foreign == 0:

                @pl.when(goes_across(step, n))
                def _():
                    ag_copy(j, 2, across).wait_send()

            else:

                @pl.when(comes_across(step, n & 3))
                def _():
                    rs_copy(j, 2, across).wait_send()

        return carry

    lax.fori_loop(1, LAST_STEP + 1, sent_step, 0)

    def own_total(late, carry):
        acc[...] = held[late]
        j = chunk_of(0, late, z)
        collect(0, late, j)

        @pl.when(crosses(late))
        def _():
            add_term(2, j, across)

        rows = pl.ds(pl.multiple_of(late * CH, CH), CH)
        dkv_v[0, rows] = (acc[0] * SCALE).astype(bf16)
        dkv_v[1, rows] = acc[1].astype(bf16)
        return carry

    lax.fori_loop(0, 2, own_total, 0)
    kv_stores = [
        pltpu.make_async_copy(dkv_v.at[n], dst.at[0], out_sem.at[4 + n]) for n, dst in enumerate((dk_hbm, dv_hbm))
    ]
    for copy in kv_stores:
        copy.start()

    for copy in short_stores + [dq_store] + kv_stores:
        copy.wait()


def emit(*refs):
    ins, outs, held, in_sem, out_sem = refs[:6], refs[6:12], refs[12:18], refs[18], refs[19]
    pieces = [(n, pl.ds(0, 1), pl.ds(half * CH, CH)) for n in (0, 1, 2) for half in (0, 1)]
    pieces += [(3, pl.ds(0, 1), pl.ds(slot, 1)) for slot in range(SLOTS)]
    pieces += [(n, pl.ds(0, 1), pl.ds(0, SLOTS)) for n in (4, 5)]
    loads = [
        pltpu.make_async_copy(ins[n].at[one, part], held[n].at[one, part], in_sem.at[i])
        for i, (n, one, part) in enumerate(pieces)
    ]
    stores = [
        pltpu.make_async_copy(held[n].at[one, part], outs[n].at[one, part], out_sem.at[i])
        for i, (n, one, part) in enumerate(pieces)
    ]
    for load in loads:
        load.start()
    for load, store in zip(loads, stores):
        load.wait()
        store.start()
    for store in stores:
        store.wait()


def body(*args):
    bf16, f32 = jnp.bfloat16, jnp.float32
    tok = args[0].shape[1]
    any_spec = pl.BlockSpec(memory_space=pltpu.HBM)
    smem_spec = pl.BlockSpec(memory_space=pltpu.SMEM)
    in_specs = [any_spec] * 5 + [smem_spec] + [any_spec] * 5 + [smem_spec] * 2
    out_shape = [jax.ShapeDtypeStruct(args[n].shape, bf16) for n in (0, 1, 2, 6, 7, 8)]
    dma = pltpu.SemaphoreType.DMA
    scratch = [
        pltpu.VMEM((NCHUNK, 2, CH, DH), bf16),
        pltpu.VMEM((tok, HC), bf16),
        pltpu.VMEM((tok, HC), bf16),
        pltpu.VMEM((tok, HC), bf16),
        pltpu.VMEM((2, DH, HC), bf16),
        pltpu.VMEM((2, DH, HC), bf16),
        pltpu.VMEM((33, CH, HC), f32),
        pltpu.VMEM((33, CH, HC), bf16),
        pltpu.VMEM((2, 8, HC), f32),
        pltpu.VMEM((2, 8, HC), f32),
        pltpu.VMEM((2, 1, HC), f32),
        pltpu.VMEM((2, 1, HC), f32),
        pltpu.VMEM((2, 1, 2 * DH), jnp.int32),
        pltpu.VMEM((2, DH, HC), f32),
        pltpu.VMEM((2, CH, DH), f32),
        pltpu.VMEM((4, 2, CH, DH), f32),
        pltpu.VMEM((NCHUNK, 2, CH, DH), bf16),
        pltpu.VMEM((3, NCHUNK, 2, CH, DH), bf16),
        pltpu.VMEM((SLOTS, CH, HC), bf16),
        pltpu.VMEM((SLOTS, CH, DH), bf16),
        pltpu.VMEM((SLOTS, CH, DH), bf16),
        pltpu.VMEM((SLOTS, CH, HC), bf16),
        pltpu.VMEM((SLOTS, CH, HC), bf16),
        pltpu.VMEM((tok, HC), bf16),
        pltpu.VMEM((2, tok, DH), bf16),
        pltpu.VMEM((SLOTS, CH, HC), bf16),
        pltpu.VMEM((SLOTS, CH, DH), bf16),
        pltpu.VMEM((SLOTS, CH, DH), bf16),
        dma((12,)),
        dma((6,)),
        dma((NCHUNK, 3)),
        dma((NCHUNK,)),
        dma((NCHUNK,)),
        dma((3, NCHUNK)),
    ]
    grads = pl.pallas_call(
        kernel,
        out_shape=out_shape,
        in_specs=in_specs,
        out_specs=[any_spec] * 6,
        scratch_shapes=scratch,
        compiler_params=pltpu.CompilerParams(
            collective_id=0, has_side_effects=True, vmem_limit_bytes=60 * 1024 * 1024
        ),
        name="attention_backward",
    )(*args)
    return tuple(
        pl.pallas_call(
            emit,
            out_shape=out_shape,
            in_specs=[any_spec] * 6,
            out_specs=[any_spec] * 6,
            scratch_shapes=[pltpu.VMEM(out.shape, bf16) for out in out_shape] + [dma((12,)), dma((12,))],
            compiler_params=pltpu.CompilerParams(vmem_limit_bytes=60 * 1024 * 1024),
            name="emit",
        )(*grads)
    )


def solution(mesh):
    seq = P("dp", "ctx", None)
    slot = P("dp", "ctx", None, None)
    return jax.shard_map(
        body,
        mesh=mesh,
        in_specs=(seq,) * 5 + (P("dp", None),) + (slot,) * 5 + (P("dp", "ctx"),) * 2,
        out_specs=(seq, seq, seq, slot, slot, slot),
        check_vma=False,
    )
```

```python
import math

import jax
import jax.numpy as jnp
from jax import lax
from jax.experimental import pallas as pl
from jax.experimental.pallas import tpu as pltpu
from jax.sharding import PartitionSpec as P

H = 6
DH = 128
CH = 128
NZ = 8
NCTX = 16
NCHUNK = 32
NDOC = 4
SLOTS = 4
HC = H * DH
PAIRS = tuple(range(0, HC, 2 * DH))
SCALE = 1.0 / math.sqrt(DH)
SCALE2 = SCALE * math.log2(math.e)
NEG = -1e30
LAST_STEP = 4

HOPS_UP = (
    {
        (0, 0, 0): (4, 3, 4, 3, 3, 2, 1, 0),
        (0, 0, 1): (0, 0, 0, 0, 0, 3, 3, 4),
        (0, 1, 0): (0, 0, 4, 3, 0, 0, 0, 3),
        (0, 1, 1): (3, 3, 0, 4, 4, 3, 4, 4),
        (1, 0, 0): (3, 3, 3, 4, 4, 4, 3, 3),
        (1, 0, 1): (0, 0, 3, 0, 0, 4, 4, 4),
        (1, 1, 0): (2, 1, 3, 4, 4, 3, 3, 3),
        (1, 1, 1): (0, 0, 0, 0, 0, 0, 0, 0),
    },
    {
        (0, 0, 0): (4, 3, 3, 4, 3, 2, 1, 0),
        (0, 0, 1): (0, 0, 0, 0, 0, 3, 4, 4),
        (0, 1, 0): (0, 0, 4, 3, 0, 0, 0, 4),
        (0, 1, 1): (4, 3, 1, 4, 4, 3, 4, 2),
        (1, 0, 0): (4, 3, 4, 3, 4, 4, 3, 3),
        (1, 0, 1): (0, 0, 3, 0, 0, 4, 3, 4),
        (1, 1, 0): (1, 4, 3, 0, 4, 3, 4, 3),
        (1, 1, 1): (0, 0, 0, 0, 0, 0, 0, 0),
    },
)
HOPS_DOWN = (
    {
        (0, 0, 0): (3, 4, 3, 4, 3, 0, 0, 0),
        (0, 0, 1): (0, 1, 2, 3, 4, 4, 4, 3),
        (0, 1, 0): (0, 0, 3, 4, 0, 3, 4, 4),
        (0, 1, 1): (4, 4, 4, 1, 1, 4, 0, 3),
        (1, 0, 0): (4, 4, 4, 3, 3, 3, 4, 4),
        (1, 0, 1): (0, 1, 2, 3, 4, 3, 3, 3),
        (1, 1, 0): (4, 4, 4, 2, 2, 4, 4, 4),
        (1, 1, 1): (0, 0, 0, 0, 0, 0, 0, 0),
    },
    {
        (0, 0, 0): (3, 4, 4, 0, 0, 0, 0, 0),
        (0, 0, 1): (0, 1, 2, 3, 4, 4, 3, 3),
        (0, 1, 0): (1, 0, 0, 4, 0, 1, 4, 3),
        (0, 1, 1): (2, 4, 4, 0, 1, 4, 1, 4),
        (1, 0, 0): (3, 4, 3, 4, 3, 3, 4, 4),
        (1, 0, 1): (3, 1, 2, 3, 4, 3, 4, 3),
        (1, 1, 0): (4, 3, 4, 4, 3, 4, 3, 4),
        (1, 1, 1): (0, 0, 0, 0, 0, 0, 0, 0),
    },
)


def needed(j, c):
    return j <= c or 15 - c <= j <= 31 - c


def device_masks(c, core):
    x, z = divmod(c, NZ)
    across = (1 - x) * NZ + z
    hops = (HOPS_UP[core], HOPS_DOWN[core])

    def chunk(plane, late, zr):
        owner = plane * NZ + zr
        return 2 * NCTX - 1 - owner if late else owner

    def over_x(plane, late, way, step, to):
        zr = (z + step if way else z - step) % NZ
        near, far = hops[way][1 - plane, 1, late][zr], hops[1 - way][1 - plane, 1, late][zr]
        there = hops[way][plane, 0, late][zr]
        return there >= step and near < step and far < NZ - step and needed(chunk(plane, late, zr), to)

    def root_over_x(plane, late, to):
        on = hops[0][1 - plane, 1, late][z] + hops[1][1 - plane, 1, late][z]
        return on >= 1 or needed(chunk(plane, late, z), to)

    has = forwards = over = root = 0
    for late in (0, 1):
        root |= root_over_x(x, late, across) << late
        root |= root_over_x(1 - x, late, c) << (2 + late)
        for way in (0, 1):
            for foreign in (0, 1):
                n = 4 * foreign + 2 * late + way
                root |= (hops[way][x, foreign, late][z] >= 1) << (4 + n)
                for step in range(1, LAST_STEP + 1):
                    zr = (z + step if way else z - step) % NZ
                    reach = hops[way][x, foreign, late][zr]
                    has |= (reach >= step) << (8 * (step - 1) + n)
                    forwards |= (reach >= step + 1) << (8 * (step - 1) + n)
            for step in range(1, LAST_STEP + 1):
                bit = 4 * (step - 1) + 2 * late + way
                over |= over_x(x, late, way, step, across) << bit
                over |= over_x(1 - x, late, way, step, c) << (16 + bit)
    return tuple(m - (1 << 32) if m >= 1 << 31 else m for m in (has, forwards, over, root))


def nt(a, b):
    return lax.dot_general(a, b, (((1,), (1,)), ((), ())), preferred_element_type=jnp.float32)


def nn(a, b):
    return lax.dot_general(a, b, (((1,), (0,)), ((), ())), preferred_element_type=jnp.float32)


def heads(ref, col):
    return jnp.concatenate([ref[:, col : col + DH], ref[:, col + DH : col + 2 * DH]], axis=0)


def row_delta(grads, outs):
    prod = grads.astype(jnp.float32) * outs.astype(jnp.float32)
    high = prod.astype(jnp.bfloat16)
    low = (prod - high.astype(jnp.float32)).astype(jnp.bfloat16)
    ones = jnp.ones((16, DH), jnp.bfloat16)
    return (nt(ones, high) + nt(ones, low))[0:1]


def kernel(
    q_hbm, k_hbm, v_hbm, o_hbm, do_hbm, doc_ref,
    qs_hbm, ks_hbm, vs_hbm, os_hbm, dos_hbm, slen_ref, scount_ref,
    dq_hbm, dk_hbm, dv_hbm, dqs_hbm, dks_hbm, dvs_hbm,
    kv, q_v, o_v, do_v, qt_v, dot_v, scores, ds_v, m_v, l_v, lse_v, delta_v, lo_v, dqt, acc, held,
    snd, rcv, qs_v, ks_v, vs_v, os_v, dos_v, dq_v, dkv_v, dqs_v, dks_v, dvs_v,
    in_sem, out_sem, ag_send, ag_recv, rs_send, rs_recv,
):
    f32, bf16 = jnp.float32, jnp.bfloat16
    c = lax.axis_index("ctx")
    x = c // NZ
    z = c - x * NZ
    late_own = 2 * NCTX - 1 - c
    z_up = lax.rem(z + 1, NZ)
    z_down = lax.rem(z + NZ - 1, NZ)
    across = (1 - x) * NZ + z
    beside = (x * NZ + z_up, x * NZ + z_down)

    core = lax.axis_index("dp") & 1
    masks = [jnp.int32(m) for m in device_masks(0, 0)]
    for device in range(1, 2 * NCTX):
        here = c + core * NCTX == device
        values = device_masks(device % NCTX, device // NCTX)
        masks = [jnp.where(here, jnp.int32(m), old) for m, old in zip(values, masks)]
    has_mask, forward_mask, over_mask, root_mask = masks

    def bit(mask, n):
        return ((mask >> n) & 1) == 1

    def has(step, n):
        return bit(has_mask, 8 * (step - 1) + n)

    def forwards(step, n):
        return bit(forward_mask, 8 * (step - 1) + n)

    def goes_across(step, n):
        return bit(over_mask, 4 * (step - 1) + n)

    def comes_across(step, n):
        return bit(over_mask, 16 + 4 * (step - 1) + n)

    def crosses(late):
        return bit(root_mask, late)

    def arrives(late):
        return bit(root_mask, 2 + late)

    def sets_out(foreign, late, way):
        return bit(root_mask, 4 + 4 * foreign + 2 * late + way)

    def choose(flag, one, zero):
        if isinstance(flag, int):
            return one if flag else zero
        return jnp.where(flag == 1, one, zero)

    def chunk_of(foreign, late, z_root):
        owner = (x + foreign * (1 - 2 * x)) * NZ + z_root
        return owner + late * (2 * NCTX - 1 - 2 * owner)

    def root_of(way, step):
        return (z + NZ + step * (2 * way - 1)) & (NZ - 1)

    def early_needs(j, who=c):
        return j <= who

    def late_needs(j, who=c):
        return (j >= 15 - who) & (j <= 2 * NCTX - 1 - who)

    def ag_copy(j, way, target):
        return pltpu.make_async_remote_copy(
            src_ref=kv.at[j], dst_ref=kv.at[j], send_sem=ag_send.at[j, way], recv_sem=ag_recv.at[j],
            device_id={"ctx": target}, device_id_type=pl.DeviceIdType.MESH,
        )

    def rs_copy(j, way, target):
        return pltpu.make_async_remote_copy(
            src_ref=snd.at[j], dst_ref=rcv.at[way, j], send_sem=rs_send.at[j], recv_sem=rs_recv.at[way, j],
            device_id={"ctx": target}, device_id_type=pl.DeviceIdType.MESH,
        )

    kv_loads = [
        pltpu.make_async_copy(src.at[0, pl.ds(half * CH, CH)], kv.at[j, which], in_sem.at[2 * which + half])
        for which, src in ((0, k_hbm), (1, v_hbm))
        for half, j in ((0, c), (1, late_own))
    ]
    long_loads = [
        pltpu.make_async_copy(src.at[0], dst, in_sem.at[4 + n])
        for n, (src, dst) in enumerate(((q_hbm, q_v), (do_hbm, do_v), (o_hbm, o_v)))
    ]
    short_loads = [
        pltpu.make_async_copy(src.at[0], dst, in_sem.at[7 + n])
        for n, (src, dst) in enumerate(
            ((qs_hbm, qs_v), (ks_hbm, ks_v), (vs_hbm, vs_v), (os_hbm, os_v), (dos_hbm, dos_v))
        )
    ]
    barrier = pltpu.get_barrier_semaphore()
    for target in beside + (across,):
        pl.semaphore_signal(
            barrier, inc=1, device_id={"ctx": target}, device_id_type=pl.DeviceIdType.MESH
        )
    for copy in kv_loads:
        copy.start()
    pl.semaphore_wait(barrier, 3)

    for copy in kv_loads:
        copy.wait()
    for late in (0, 1):
        j = chunk_of(0, late, z)

        @pl.when(crosses(late))
        def _():
            ag_copy(j, 2, across).start()

    for late in (0, 1):
        j = chunk_of(0, late, z)
        for way in (0, 1):

            @pl.when(sets_out(0, late, way))
            def _():
                ag_copy(j, way, beside[way]).start()

    for copy in long_loads + short_loads:
        copy.start()
    for copy in long_loads:
        copy.wait()
    halves = [(pl.ds(half * CH, CH), own_chunk) for half, own_chunk in ((0, c), (1, late_own))]
    ends = []
    total = doc_ref[0, 0]
    for d in range(NDOC):
        ends.append(total)
        if d + 1 < NDOC:
            total = total + doc_ref[0, d + 1]
    lane = lax.rem(lax.broadcasted_iota(jnp.int32, (1, 2 * DH), 1), CH)
    sub = lax.broadcasted_iota(jnp.int32, (CH, 1), 0)
    for half, (rows, own_chunk) in enumerate(halves):
        pos = own_chunk * CH + lane
        first = jnp.zeros((1, 2 * DH), jnp.int32)
        for end in ends:
            first = jnp.maximum(first, jnp.where(pos >= end, end, 0))
        lo_v[half] = first
        for col in PAIRS:
            delta_v[half, :, col : col + 2 * DH] = row_delta(heads(do_v.at[rows], col), heads(o_v.at[rows], col))
        for col in range(0, HC, DH):
            qt_v[half, :, col : col + DH] = q_v[rows, col : col + DH].T
            dot_v[half, :, col : col + DH] = do_v[rows, col : col + DH].T
        m_v[half] = jnp.full((8, HC), NEG, f32)
        l_v[half] = jnp.zeros((8, HC), f32)
    dqt[0] = jnp.zeros((DH, HC), f32)

    def slot_of(half, j):
        return j if half == 0 else NCTX + j - (15 - c)

    def score_tiles(which, j):
        keys = kv[j, 0]
        key_pos = j * CH + sub
        for half in which:
            own_chunk = halves[half][1]
            visible = (key_pos >= lo_v[half]) & (key_pos <= own_chunk * CH + lane)
            bias = jnp.where(visible, 0.0, NEG)
            slot = slot_of(half, j)
            for col in PAIRS:
                cols = slice(col, col + 2 * DH)
                s = nn(keys, qt_v[half, :, cols]) * SCALE2 + bias
                scores[slot, :, cols] = s
                s = s.reshape(CH // 8, 8, 2 * DH)
                m_old = m_v[half, :, cols]
                m_new = jnp.maximum(m_old, jnp.max(s, axis=0))
                m_v[half, :, cols] = m_new
                l_v[half, :, cols] = l_v[half, :, cols] * jnp.exp2(m_old - m_new) + jnp.sum(
                    jnp.exp2(s - m_new[None]), axis=0
                )

    def for_needed(j, has, tiles):
        early, late = early_needs(j), late_needs(j)
        for which, wanted in (((0, 1), early & late), ((0,), early & ~late), ((1,), late & ~early)):

            @pl.when(has & wanted)
            def _():
                tiles(which, j)

    def score_item(j, has):
        for_needed(j, has, score_tiles)

    def short_slot(slot):
        length = jnp.where(slot < scount_ref[0, 0], slen_ref[0, slot], 0)
        keys = ks_v[slot]
        values = vs_v[slot]
        visible = (sub <= lane) & (lane < length)
        dk = jnp.zeros((CH, DH), f32)
        dv = jnp.zeros((CH, DH), f32)
        for col in PAIRS:
            queries = heads(qs_v.at[slot], col)
            grads = heads(dos_v.at[slot], col)
            delta = row_delta(grads, heads(os_v.at[slot], col))
            s = jnp.where(visible, nt(keys, queries) * SCALE2, NEG)
            e = jnp.exp2(s - jnp.max(s, axis=0, keepdims=True))
            inverse = jnp.where(lane < length, 1.0 / jnp.sum(e, axis=0, keepdims=True), 0.0)
            p = e * inverse
            ds = (p * (nt(values, grads) - delta)).astype(bf16)
            dv = dv + nn(p.astype(bf16), grads)
            dk = dk + nn(ds, queries)
            dq = lax.dot_general(keys, ds, (((0,), (0,)), ((), ())), preferred_element_type=f32)
            for n in (0, 1):
                dqs_v[slot, :, col + n * DH : col + (n + 1) * DH] = (
                    dq[:, n * DH : (n + 1) * DH].T * SCALE
                ).astype(bf16)
        dks_v[slot] = (dk * SCALE).astype(bf16)
        dvs_v[slot] = dv.astype(bf16)

    score_item(c, c >= 0)
    score_item(late_own, c >= 0)

    for late in (0, 1):
        j = chunk_of(1, late, z)

        @pl.when(arrives(late))
        def _():
            ag_copy(j, 2, across).wait_recv()
            for way in (0, 1):

                @pl.when(sets_out(1, late, way))
                def _():
                    ag_copy(j, way, beside[way]).start()

    def foreign_score(late, carry):
        score_item(chunk_of(1, late, z), arrives(late))
        return carry

    lax.fori_loop(0, 2, foreign_score, 0)

    for copy in short_loads:
        copy.wait()

    def score_across(step):
        def item(n, carry):
            j = chunk_of(1, n // 2, root_of(lax.rem(n, 2), step))

            @pl.when(comes_across(step, n))
            def _():
                ag_copy(j, 2, across).wait_recv()
                score_item(j, c >= 0)

            return carry

        @pl.when(step >= 1)
        def _():
            lax.fori_loop(0, 4, item, 0)

    def gather_step(step, carry):
        def pair(q, carry):
            foreign, late = q // 2, q & 1
            for way in (0, 1):
                j = chunk_of(foreign, late, root_of(way, step))

                @pl.when(has(step, 2 * q + way))
                def _():
                    ag_copy(j, way, beside[way]).wait_recv()

                @pl.when(forwards(step, 2 * q + way))
                def _():
                    ag_copy(j, way, beside[way]).start()

                @pl.when((foreign == 0) & goes_across(step, (2 * q + way) & 3))
                def _():
                    ag_copy(j, 2, across).start()

            @pl.when(q == 0)
            def _():
                short_slot(step - 1)

            def item(way, carry):
                score_item(chunk_of(foreign, late, root_of(way, step)), has(step, 2 * q + way))
                return carry

            return lax.fori_loop(0, 2, item, carry)

        lax.fori_loop(0, 4, pair, carry)
        score_across(step - 1)
        return carry

    lax.fori_loop(1, LAST_STEP + 1, gather_step, 0)
    score_across(LAST_STEP)

    short_stores = [
        pltpu.make_async_copy(src, dst.at[0], out_sem.at[n])
        for n, (src, dst) in enumerate(((dqs_v, dqs_hbm), (dks_v, dks_hbm), (dvs_v, dvs_hbm)))
    ]
    for copy in short_stores:
        copy.start()

    for half in (0, 1):
        m = jnp.max(m_v[half], axis=0, keepdims=True)
        lse_v[half] = m + jnp.log2(jnp.sum(l_v[half] * jnp.exp2(m_v[half] - m), axis=0, keepdims=True))

    def grad_tiles(which, j):
        values = kv[j, 1]
        p_parts, ds_parts, q_parts, do_parts = [], [], [], []
        for half in which:
            rows, own_chunk = halves[half]
            slot = slot_of(half, j)
            for col in PAIRS:
                cols = slice(col, col + 2 * DH)
                grads = heads(do_v.at[rows], col)
                p = jnp.exp2(scores[slot, :, cols] - lse_v[half, :, cols])
                ds = (p * (nn(values, dot_v[half, :, cols]) - delta_v[half, :, cols])).astype(bf16)
                ds_v[slot, :, cols] = ds
                p_parts.append(p.astype(bf16))
                ds_parts.append(ds)
                q_parts.append(heads(q_v.at[rows], col))
                do_parts.append(grads)
        acc[0] = nn(jnp.concatenate(ds_parts, axis=1), jnp.concatenate(q_parts, axis=0))
        acc[1] = nn(jnp.concatenate(p_parts, axis=1), jnp.concatenate(do_parts, axis=0))

    def grad_item(j):
        @pl.when(~(early_needs(j) | late_needs(j)))
        def _():
            acc[...] = jnp.zeros((2, CH, DH), f32)

        for_needed(j, c >= 0, grad_tiles)

    def grads_across(step):
        def item(n, carry):
            j = chunk_of(1, n // 2, root_of(lax.rem(n, 2), step))

            @pl.when(comes_across(step, n))
            def _():
                grad_item(j)
                snd[j] = acc[...].astype(bf16)
                rs_copy(j, 2, across).start()

            return carry

        @pl.when(step >= 1)
        def _():
            lax.fori_loop(0, 4, item, 0)

    def add_term(way, j, target):
        rs_copy(j, way, target).wait_recv()
        acc[...] += rcv[way, j].astype(f32)

    def grads_of_roots(n, carry):
        foreign, late = n // 2, n & 1

        @pl.when((foreign == 0) | arrives(late))
        def _():
            grad_item(chunk_of(foreign, late, z))
            held[n] = acc[...]

        return carry

    def scatter_step(back, carry):
        step = LAST_STEP - back

        @pl.when(step == 1)
        def _():
            lax.fori_loop(0, 4, grads_of_roots, 0)

        grads_across(step - 1)

        def item(i, carry):
            n = (i + 4) & 7
            foreign, late, way = n // 4, (n // 2) & 1, n & 1
            j = chunk_of(foreign, late, root_of(way, step))

            @pl.when(has(step, n))
            def _():
                grad_item(j)

                @pl.when(forwards(step, n))
                def _():
                    add_term(way, j, beside[0])

                @pl.when((foreign == 0) & goes_across(step, n & 3))
                def _():
                    add_term(2, j, across)

                snd[j] = acc[...].astype(bf16)
                rs_copy(j, way, choose(way, beside[0], beside[1])).start()

            return carry

        return lax.fori_loop(0, 8, item, carry)

    grads_across(LAST_STEP)
    lax.fori_loop(0, LAST_STEP, scatter_step, 0)

    def collect(foreign, late, j):
        for way in (0, 1):

            @pl.when(sets_out(foreign, late, way))
            def _():
                add_term(way, j, beside[way])

    def foreign_root(late, carry):
        j = chunk_of(1, late, z)

        @pl.when(arrives(late))
        def _():
            acc[...] = held[2 + late]
            collect(1, late, j)
            snd[j] = acc[...].astype(bf16)
            rs_copy(j, 2, across).start()

        return carry

    lax.fori_loop(0, 2, foreign_root, 0)

    def tn(a, b):
        return lax.dot_general(a, b, (((0,), (0,)), ((), ())), preferred_element_type=f32)

    def dq_early(first, count):
        keys = kv[pl.ds(first, count), 0].reshape(count * CH, DH)
        for col in PAIRS:
            cols = slice(col, col + 2 * DH)
            dqt[0, :, cols] += tn(keys, ds_v[pl.ds(first, count), :, cols].reshape(count * CH, 2 * DH))

    def dq_early_two(n, carry):
        dq_early(2 * n, 2)
        return carry

    lax.fori_loop(0, (c + 1) // 2, dq_early_two, 0)

    @pl.when(lax.rem(c, 2) == 0)
    def _():
        dq_early(c, 1)

    keys = kv[pl.ds(15 - c, 17), 0].reshape(17 * CH, DH)
    for col in PAIRS:
        cols = slice(col, col + 2 * DH)
        dqt[1, :, cols] = tn(keys, ds_v[NCTX : NCTX + 17, :, cols].reshape(17 * CH, 2 * DH))
    for half, (rows, own_chunk) in enumerate(halves):
        for col in range(0, HC, DH):
            dq_v[rows, col : col + DH] = (dqt[half, :, col : col + DH].T * SCALE).astype(bf16)
    dq_store = pltpu.make_async_copy(dq_v, dq_hbm.at[0], out_sem.at[3])
    dq_store.start()

    for late in (0, 1):
        j = chunk_of(0, late, z)

        @pl.when(crosses(late))
        def _():
            ag_copy(j, 2, across).wait_send()

        for foreign in (0, 1):
            j = chunk_of(foreign, late, z)
            for way in (0, 1):

                @pl.when(sets_out(foreign, late, way))
                def _():
                    ag_copy(j, way, beside[way]).wait_send()

        @pl.when(arrives(late))
        def _():
            rs_copy(chunk_of(1, late, z), 2, across).wait_send()

    def sent_step(step, carry):
        for n in range(8):
            foreign, late, way = n // 4, n // 2 % 2, n % 2
            j = chunk_of(foreign, late, root_of(way, step))

            @pl.when(has(step, n))
            def _():
                rs_copy(j, way, beside[0]).wait_send()

            @pl.when(forwards(step, n))
            def _():
                ag_copy(j, way, beside[0]).wait_send()

            if foreign == 0:

                @pl.when(goes_across(step, n))
                def _():
                    ag_copy(j, 2, across).wait_send()

            else:

                @pl.when(comes_across(step, n & 3))
                def _():
                    rs_copy(j, 2, across).wait_send()

        return carry

    lax.fori_loop(1, LAST_STEP + 1, sent_step, 0)

    def own_total(late, carry):
        acc[...] = held[late]
        j = chunk_of(0, late, z)
        collect(0, late, j)

        @pl.when(crosses(late))
        def _():
            add_term(2, j, across)

        rows = pl.ds(pl.multiple_of(late * CH, CH), CH)
        dkv_v[0, rows] = (acc[0] * SCALE).astype(bf16)
        dkv_v[1, rows] = acc[1].astype(bf16)
        return carry

    lax.fori_loop(0, 2, own_total, 0)
    kv_stores = [
        pltpu.make_async_copy(dkv_v.at[n], dst.at[0], out_sem.at[4 + n]) for n, dst in enumerate((dk_hbm, dv_hbm))
    ]
    for copy in kv_stores:
        copy.start()

    for copy in short_stores + [dq_store] + kv_stores:
        copy.wait()


def emit(*refs):
    ins, outs, held, in_sem, out_sem = refs[:6], refs[6:12], refs[12:18], refs[18], refs[19]
    pieces = [(n, pl.ds(0, 1), pl.ds(half * CH, CH)) for n in (0, 1, 2) for half in (0, 1)]
    pieces += [(3, pl.ds(0, 1), pl.ds(slot, 1)) for slot in range(SLOTS)]
    pieces += [(n, pl.ds(0, 1), pl.ds(0, SLOTS)) for n in (4, 5)]
    loads = [
        pltpu.make_async_copy(ins[n].at[one, part], held[n].at[one, part], in_sem.at[i])
        for i, (n, one, part) in enumerate(pieces)
    ]
    stores = [
        pltpu.make_async_copy(held[n].at[one, part], outs[n].at[one, part], out_sem.at[i])
        for i, (n, one, part) in enumerate(pieces)
    ]
    for load in loads:
        load.start()
    for load, store in zip(loads, stores):
        load.wait()
        store.start()
    for store in stores:
        store.wait()


def body(*args):
    bf16, f32 = jnp.bfloat16, jnp.float32
    tok = args[0].shape[1]
    any_spec = pl.BlockSpec(memory_space=pltpu.HBM)
    smem_spec = pl.BlockSpec(memory_space=pltpu.SMEM)
    in_specs = [any_spec] * 5 + [smem_spec] + [any_spec] * 5 + [smem_spec] * 2
    out_shape = [jax.ShapeDtypeStruct(args[n].shape, bf16) for n in (0, 1, 2, 6, 7, 8)]
    dma = pltpu.SemaphoreType.DMA
    scratch = [
        pltpu.VMEM((NCHUNK, 2, CH, DH), bf16),
        pltpu.VMEM((tok, HC), bf16),
        pltpu.VMEM((tok, HC), bf16),
        pltpu.VMEM((tok, HC), bf16),
        pltpu.VMEM((2, DH, HC), bf16),
        pltpu.VMEM((2, DH, HC), bf16),
        pltpu.VMEM((33, CH, HC), f32),
        pltpu.VMEM((33, CH, HC), bf16),
        pltpu.VMEM((2, 8, HC), f32),
        pltpu.VMEM((2, 8, HC), f32),
        pltpu.VMEM((2, 1, HC), f32),
        pltpu.VMEM((2, 1, HC), f32),
        pltpu.VMEM((2, 1, 2 * DH), jnp.int32),
        pltpu.VMEM((2, DH, HC), f32),
        pltpu.VMEM((2, CH, DH), f32),
        pltpu.VMEM((4, 2, CH, DH), f32),
        pltpu.VMEM((NCHUNK, 2, CH, DH), bf16),
        pltpu.VMEM((3, NCHUNK, 2, CH, DH), bf16),
        pltpu.VMEM((SLOTS, CH, HC), bf16),
        pltpu.VMEM((SLOTS, CH, DH), bf16),
        pltpu.VMEM((SLOTS, CH, DH), bf16),
        pltpu.VMEM((SLOTS, CH, HC), bf16),
        pltpu.VMEM((SLOTS, CH, HC), bf16),
        pltpu.VMEM((tok, HC), bf16),
        pltpu.VMEM((2, tok, DH), bf16),
        pltpu.VMEM((SLOTS, CH, HC), bf16),
        pltpu.VMEM((SLOTS, CH, DH), bf16),
        pltpu.VMEM((SLOTS, CH, DH), bf16),
        dma((12,)),
        dma((6,)),
        dma((NCHUNK, 3)),
        dma((NCHUNK,)),
        dma((NCHUNK,)),
        dma((3, NCHUNK)),
    ]
    grads = pl.pallas_call(
        kernel,
        out_shape=out_shape,
        in_specs=in_specs,
        out_specs=[any_spec] * 6,
        scratch_shapes=scratch,
        compiler_params=pltpu.CompilerParams(
            collective_id=0, has_side_effects=True, vmem_limit_bytes=60 * 1024 * 1024
        ),
        name="attention_backward",
    )(*args)
    return tuple(
        pl.pallas_call(
            emit,
            out_shape=out_shape,
            in_specs=[any_spec] * 6,
            out_specs=[any_spec] * 6,
            scratch_shapes=[pltpu.VMEM(out.shape, bf16) for out in out_shape] + [dma((12,)), dma((12,))],
            compiler_params=pltpu.CompilerParams(vmem_limit_bytes=60 * 1024 * 1024),
            name="emit",
        )(*grads)
    )


def solution(mesh):
    seq = P("dp", "ctx", None)
    slot = P("dp", "ctx", None, None)
    return jax.shard_map(
        body,
        mesh=mesh,
        in_specs=(seq,) * 5 + (P("dp", None),) + (slot,) * 5 + (P("dp", "ctx"),) * 2,
        out_specs=(seq, seq, seq, slot, slot, slot),
        check_vma=False,
    )
```
